128 devices in a mesh: dp: 4 (over y), ep: 32 (over z, x, core).
Axes of the slice: x: 4, y: 4, z: 4, core: 2. Of those that a mesh axis runs over, the one named last changes fastest.
Arguments:
- residual: bfloat16 [2048, 4096], P(('dp', 'ep')), may hold values from -1.1953125 to 1.1953125
- query: bfloat16 [2048, 4096], P(('dp', 'ep')), may hold values from -6 to 6
- new_key_value: bfloat16 [2048, 2, 256], P(('dp', 'ep')), may hold values from -6 to 6
- cached_key_rows: bfloat16 [2048, 256, 256], P(('dp', 'ep')), may hold values from -64 to 64
- cached_value_rows: bfloat16 [2048, 256, 256], P(('dp', 'ep')), may hold values from -6 to 6
- lengths: int32 [2048], P(('dp', 'ep')), may hold values from 1 to 256, as said below
- q_gain: float32 [128], replicated, may hold values from 0.1 to 1.9
- k_gain: float32 [128], replicated, may hold values from 0.1 to 1.9
- out_weight: bfloat16 [4096, 4096], P(None, 'ep'), may hold values from -0.09375 to 0.09375
- moe_gain: float32 [4096], replicated, may hold values from 0.1 to 1.9
- expert_ids: int32 [2048, 8], P(('dp', 'ep')), may hold values from 0 to 127, all different within a row; in each aligned block of 16 rows (0 to 15, 16 to 31, ...) at most 2 rows name the same one
- gate_probs: float32 [2048, 8], P(('dp', 'ep')), may hold values from 0.02 to 1
- expert_gate_up: bfloat16 [128, 4096, 1536], P(('dp', 'ep')), may hold values from -0.09375 to 0.09375
- expert_down: bfloat16 [128, 768, 4096], P(('dp', 'ep')), may hold values from -0.21875 to 0.21875
Outputs:
- attended: bfloat16 [2048, 4096], P(('dp', 'ep'))
- mixed: bfloat16 [2048, 4096], P(('dp', 'ep'))
The draws below stay inside these ranges and needn't reach their ends.
Inputs may be any that keep to these rules, and one draw needn't show every extreme that they name: `expert_ids`: each token names 8 different experts; among the 16 tokens of one device no expert is named more than 2 times. `lengths`: some request has exactly 256 live slots in every draw.
All inputs are finite; a program needn't handle non-finite values.
Results may differ from the reference program's by a relative error of at most 0.02.
Values may be sent and summed in bfloat16 or wider, within the bound.
A program may use at most 128 MiB of HBM per device.

```python
import math
import jax
import jax.numpy as jnp
import numpy as np
from jax import lax

D = 4096
QUERY_HEADS = 32
KEY_VALUE_HEADS = 2
HEAD_SIZE = 128
FF = 768
TOP = 8
TOKENS_PER_CHIP = 16
CACHE_SLOTS = 256
EXPERTS = 128
REQUEST_TOTAL = 2048
CAP = 2
N_DP = 4
N_EP = 32


def shared_base(key):
    return jax.random.normal(jax.random.fold_in(key, 101), (REQUEST_TOTAL, KEY_VALUE_HEADS, HEAD_SIZE), jnp.float32)


def draw_query(key, part):
    base_offset = shared_base(key)
    key = jax.random.fold_in(key, 1)
    random_noise = jax.random.normal(key, (REQUEST_TOTAL, KEY_VALUE_HEADS, QUERY_HEADS // KEY_VALUE_HEADS, HEAD_SIZE), jnp.float32)
    value_rows = 0.6 * base_offset[:, :, None, :] + 0.8 * random_noise
    return jnp.clip(value_rows, -6.0, 6.0).reshape(REQUEST_TOTAL, QUERY_HEADS * HEAD_SIZE).astype(jnp.bfloat16)


def draw_new_key_value(key, part):
    base_offset = shared_base(key)
    key = jax.random.fold_in(key, 2)
    first_part, second_part = jax.random.split(key)
    fresh_keys = 0.6 * base_offset + 0.8 * jax.random.normal(first_part, (REQUEST_TOTAL, KEY_VALUE_HEADS, HEAD_SIZE), jnp.float32)
    fresh_values = jax.random.normal(second_part, (REQUEST_TOTAL, KEY_VALUE_HEADS, HEAD_SIZE), jnp.float32)
    stacked_rows = jnp.stack([jnp.clip(fresh_keys, -6.0, 6.0), jnp.clip(fresh_values, -6.0, 6.0)], axis=1)
    return stacked_rows.reshape(REQUEST_TOTAL, 2, KEY_VALUE_HEADS * HEAD_SIZE).astype(jnp.bfloat16)


def draw_cached_key_rows(key, part):
    key = jax.random.fold_in(key, 3)
    first_part = jax.random.fold_in(key, 0)
    random_noise = jax.random.normal(first_part, (REQUEST_TOTAL, CACHE_SLOTS, KEY_VALUE_HEADS, HEAD_SIZE), jnp.float32)
    value_rows = jnp.clip(random_noise, -6.0, 6.0)
    return value_rows.reshape(REQUEST_TOTAL, CACHE_SLOTS, KEY_VALUE_HEADS * HEAD_SIZE).astype(jnp.bfloat16)


def draw_lengths(key, part):
    key = jax.random.fold_in(key, 4)
    first_part, second_part, third_part, fourth = jax.random.split(key, 4)
    groups = REQUEST_TOTAL // TOKENS_PER_CHIP
    longest = jax.random.randint(first_part, (groups,), max(1, CACHE_SLOTS // 8), CACHE_SLOTS + 1)
    chosen = jax.random.randint(second_part, (), 0, groups)
    longest = jnp.where(jnp.arange(groups) == chosen, CACHE_SLOTS, longest)
    drawn = jax.random.randint(third_part, (groups, TOKENS_PER_CHIP), 1, longest[:, None] + 1)
    place = jax.random.randint(fourth, (groups, 1), 0, TOKENS_PER_CHIP)
    drawn = jnp.where(jnp.arange(TOKENS_PER_CHIP)[None, :] == place, longest[:, None], drawn)
    return drawn.reshape(REQUEST_TOTAL).astype(jnp.int32)


def block_levels(own_key, extent, pieces, low, largest):
    level, own = 1.0, jax.random.fold_in(own_key, 6)
    for axis_at, shards_of in pieces:
        steps = jnp.exp(jax.random.uniform(jax.random.fold_in(own, axis_at), (shards_of,), jnp.float32, low / len(pieces), largest / len(pieces)))
        level = level * jnp.repeat(steps, extent[axis_at] // shards_of).reshape([-1 if axis == axis_at else 1 for axis in range(len(extent))])
    return level


def deal_out(stream_key, own, number, rows, number_of, top, most, lean):
    ranking = jax.random.permutation(stream_key, number_of)
    crowded, ordinary = portions_of(number_of, rows * top, most, lean, True), portions_of(number_of, rows * top, most, lean, False)
    places = jnp.arange(number_of)

    def named(tallies, rotation):
        used = int((tallies > 0).sum())
        fixed = max(1, used // 4)
        shifted = fixed + (places - fixed + rotation * (used - fixed)) % max(1, number_of - fixed)
        return jnp.zeros((number_of,), jnp.int32).at[ranking[jnp.where(places < fixed, places, shifted)]].set(jnp.asarray(tallies, jnp.int32))

    tallies = jnp.where(number % 4 == 0, named(crowded, number // 4), named(ordinary, number - number // 4 - 1))
    mixed = jax.random.permutation(jax.random.fold_in(own, 3), number_of)
    source_of, sink = mixed[0:number_of // 2 * 2:2], mixed[1:number_of // 2 * 2:2]
    margin = jnp.minimum(tallies[source_of] - 1, most - tallies[sink]) // 2
    margin = jnp.where((source_of == ranking[0]) | (sink == ranking[0]) | (tallies[sink] == 0), 0, jnp.maximum(margin, 0))
    shifted = jax.random.randint(jax.random.fold_in(own, 4), (number_of // 2,), 0, 1 << 20) % (margin + 1)
    tallies = tallies.at[source_of].add(-shifted).at[sink].add(shifted)
    labels = jnp.searchsorted(jnp.cumsum(tallies), jnp.arange(rows * top), side="right").astype(jnp.int32)
    listing = labels.reshape(top, rows).T
    listing = listing[jax.random.permutation(jax.random.fold_in(own, 1), rows)]
    rotation = jax.random.randint(jax.random.fold_in(own, 2), (rows, 1), 0, top)
    return jnp.take_along_axis(listing, (jnp.arange(top)[None, :] + rotation) % top, axis=1)


def portions_of(amount, total, reach, slope, full):
    weights = [(1 << 20) // math.isqrt(rank ** slope) + 1 for rank in range(1, amount + 1)]
    largest = reach if full else min(reach, max(-(-total // amount), total * weights[0] // sum(weights)))
    least = 1 if total - largest >= amount - 1 else 0
    holding, rest = [largest] + [least] * (amount - 1), total - largest - least * (amount - 1)
    while rest > 0:
        free = [i for i in range(1, amount) if holding[i] < largest] or [i for i in range(1, amount) if holding[i] < reach]
        pool, budget = sum([weights[i] for i in free]), rest
        for i in free:
            extra = min(reach - holding[i], max(1, budget * weights[i] // pool), rest)
            holding[i] = holding[i] + extra
            rest = rest - extra
    return np.array(holding)


def noise(own_key, dims, scale, limit, cuts=(), held_as=jnp.bfloat16):
    entries = scale * jax.random.normal(own_key, dims, jnp.float32)
    if cuts:
        entries = entries * block_levels(own_key, dims, cuts, -0.22, 0.18)
    return jnp.clip(entries, -limit, limit).astype(held_as)


def setup_inputs(seed: int = 0) -> dict:
    arg_keys = jax.random.split(jax.random.key(seed), 15)
    residual = noise(arg_keys[0], (REQUEST_TOTAL, D), 0.2, 1.1953125, ((0, 128),))
    query = draw_query(jax.random.fold_in(arg_keys[14], 71), 0)
    new_key_value = draw_new_key_value(jax.random.fold_in(arg_keys[14], 71), 0)
    cached_key_rows = draw_cached_key_rows(jax.random.fold_in(arg_keys[14], 71), 0)
    cached_value_rows = noise(arg_keys[4], (REQUEST_TOTAL, CACHE_SLOTS, KEY_VALUE_HEADS * HEAD_SIZE), 1.0, 6.0, ((0, 128),))
    lengths = draw_lengths(jax.random.fold_in(arg_keys[14], 71), 0)
    q_gain = jnp.clip(1.0 + 0.18 * jax.random.normal(arg_keys[6], (HEAD_SIZE,), jnp.float32), 0.1, 1.9)
    k_gain = jnp.clip(1.0 + 0.18 * jax.random.normal(arg_keys[7], (HEAD_SIZE,), jnp.float32), 0.1, 1.9)
    out_weight = noise(arg_keys[8], (QUERY_HEADS * HEAD_SIZE, D), (QUERY_HEADS * HEAD_SIZE) ** -0.5, 0.09375, ((1, 32),))
    moe_gain = jnp.clip(1.0 + 0.18 * jax.random.normal(arg_keys[9], (D,), jnp.float32), 0.1, 1.9)
    expert_ids_keys = jax.random.split(jax.random.fold_in(arg_keys[10], 1), REQUEST_TOTAL // TOKENS_PER_CHIP)
    expert_ids_turns = jax.random.permutation(jax.random.fold_in(arg_keys[10], 3), REQUEST_TOTAL // TOKENS_PER_CHIP)
    expert_ids = jax.vmap(lambda own, number: deal_out(jax.random.fold_in(arg_keys[10], 2), own, number, TOKENS_PER_CHIP, EXPERTS, TOP, CAP, 2))(expert_ids_keys, expert_ids_turns).reshape((REQUEST_TOTAL, TOP))
    gate_probs = jnp.clip(jnp.exp(math.log(1.0) - 3.912023 * jax.random.uniform(arg_keys[11], (REQUEST_TOTAL, TOP), jnp.float32) ** block_levels(arg_keys[11], (REQUEST_TOTAL, TOP), ((0, 128),), -0.2, 0.2)), 0.02, 1.0)
    expert_gate_up = noise(arg_keys[12], (EXPERTS, D, 2 * FF), D ** -0.5, 0.09375, ((0, 128),))
    expert_down = noise(arg_keys[13], (EXPERTS, FF, D), FF ** -0.5, 0.21875, ((0, 128),))
    return {"residual": residual, "query": query, "new_key_value": new_key_value, "cached_key_rows": cached_key_rows, "cached_value_rows": cached_value_rows, "lengths": lengths, "q_gain": q_gain, "k_gain": k_gain, "out_weight": out_weight, "moe_gain": moe_gain, "expert_ids": expert_ids, "gate_probs": gate_probs, "expert_gate_up": expert_gate_up, "expert_down": expert_down}


EPSILON = 1e-06
THETA = 1000000.0

def head_norm(value_rows, gain):
    mean_square = lax.optimization_barrier(jnp.mean(value_rows * value_rows, axis=-1, keepdims=True))
    return value_rows * lax.rsqrt(mean_square + EPSILON) * gain

def rotate(value_rows, positions):
    width = value_rows.shape[-1]
    half = width // 2
    steps = jnp.arange(half).astype(jnp.float32)
    freqs = jnp.exp(steps * (-2.0 * math.log(THETA) / width))
    angles = positions[..., None] * freqs
    cosines = jnp.cos(angles)
    sines = jnp.sin(angles)
    first_part = value_rows[..., :half]
    second_part = value_rows[..., half:]
    return jnp.concatenate([first_part * cosines - second_part * sines, second_part * cosines + first_part * sines], axis=-1)

def attend_block(query, new_key_value, cached_key_rows, cached_value_rows, lengths, q_gain, k_gain):
    head = q_gain.shape[0]
    count = query.shape[0]
    kv_heads = new_key_value.shape[2] // head
    group = query.shape[1] // head // kv_heads
    slots = cached_key_rows.shape[1]
    positions = lengths.astype(jnp.float32)
    queries = query.astype(jnp.float32).reshape(count, kv_heads, group, head)
    queries = rotate(head_norm(queries, q_gain), positions[:, None, None]).astype(jnp.bfloat16)
    new_key = new_key_value[:, 0].astype(jnp.float32).reshape(count, kv_heads, head)
    new_key = rotate(head_norm(new_key, k_gain), positions[:, None]).astype(jnp.bfloat16)
    new_value = new_key_value[:, 1].reshape(count, kv_heads, head)
    stored_keys = cached_key_rows.reshape(count, slots, kv_heads, head)
    stored_values = cached_value_rows.reshape(count, slots, kv_heads, head)
    scale = 1.0 / math.sqrt(head)
    scores = jnp.einsum('tkgd,tckd->tkgc', queries.astype(jnp.float32), stored_keys.astype(jnp.float32)) * scale
    own_score = jnp.einsum('tkgd,tkd->tkg', queries.astype(jnp.float32), new_key.astype(jnp.float32)) * scale
    live = (jnp.arange(slots)[None, :] < lengths[:, None])[:, None, None, :]
    scores = jnp.where(live, scores, -jnp.inf)
    highest = jnp.maximum(lax.optimization_barrier(jnp.max(scores, axis=-1)), own_score)
    expos = jnp.where(live, jnp.exp(scores - highest[..., None]), 0.0)
    own_expo = jnp.exp(own_score - highest)
    total = lax.optimization_barrier(jnp.sum(expos, axis=-1)) + own_expo
    probs = (expos / total[..., None]).astype(jnp.bfloat16)
    own_prob = (own_expo / total).astype(jnp.bfloat16)
    summed = jnp.einsum('tkgc,tckd->tkgd', probs.astype(jnp.float32), stored_values.astype(jnp.float32))
    summed = summed + own_prob.astype(jnp.float32)[..., None] * new_value.astype(jnp.float32)[:, :, None, :]
    return summed.astype(jnp.bfloat16).reshape(count, kv_heads * group * head)

def expert_rows(rows, gate_up, down):
    hidden_size = down.shape[0]
    both = jnp.dot(rows, gate_up, preferred_element_type=jnp.float32)
    activated = (jax.nn.silu(both[:, :hidden_size]) * both[:, hidden_size:]).astype(jnp.bfloat16)
    return jnp.dot(activated, down, preferred_element_type=jnp.float32)

def reference(residual, query, new_key_value, cached_key_rows, cached_value_rows, lengths, q_gain, k_gain, out_weight, moe_gain, expert_ids, gate_probs, expert_gate_up, expert_down):
    block_list = REQUEST_TOTAL // TOKENS_PER_CHIP

    def single_block(items):
        return attend_block(items[0], items[1], items[2], items[3], items[4], q_gain, k_gain)
    head_list = lax.map(single_block, (query.reshape(block_list, TOKENS_PER_CHIP, QUERY_HEADS * HEAD_SIZE), new_key_value.reshape(block_list, TOKENS_PER_CHIP, 2, KEY_VALUE_HEADS * HEAD_SIZE), cached_key_rows.reshape(block_list, TOKENS_PER_CHIP, CACHE_SLOTS, KEY_VALUE_HEADS * HEAD_SIZE), cached_value_rows.reshape(block_list, TOKENS_PER_CHIP, CACHE_SLOTS, KEY_VALUE_HEADS * HEAD_SIZE), lengths.reshape(block_list, TOKENS_PER_CHIP)))
    head_list = head_list.reshape(REQUEST_TOTAL, QUERY_HEADS * HEAD_SIZE)
    projected = jnp.dot(head_list, out_weight, preferred_element_type=jnp.float32).astype(jnp.bfloat16)
    attended = (residual.astype(jnp.float32) + projected.astype(jnp.float32)).astype(jnp.bfloat16)
    stream = attended.astype(jnp.float32)
    normed = (stream * lax.rsqrt(lax.optimization_barrier(jnp.mean(stream * stream, axis=-1, keepdims=True)) + EPSILON) * moe_gain).astype(jnp.bfloat16)
    weights = gate_probs / lax.optimization_barrier(jnp.sum(gate_probs, axis=-1, keepdims=True))
    flat_ids = expert_ids.reshape(-1)
    flat_weights = weights.reshape(-1)
    most = N_DP * N_EP * CAP

    def one_expert(total, expert):
        matches = flat_ids == expert
        found = jnp.nonzero(matches, size=most, fill_value=0)[0].astype(jnp.int32)
        valid = jnp.arange(most) < jnp.sum(matches.astype(jnp.int32))
        owners = found // TOP
        result = expert_rows(normed[owners], expert_gate_up[expert], expert_down[expert])
        scaled = result * jnp.where(valid, flat_weights[found], 0.0)[:, None]
        return (total.at[owners].add(scaled), None)
    moe_out, _ = lax.scan(one_expert, jnp.zeros((REQUEST_TOTAL, D), jnp.float32), jnp.arange(EXPERTS).astype(jnp.int32))
    mixed = (stream + moe_out).astype(jnp.bfloat16)
    return (attended, mixed)
```

```python
import math

import jax
import jax.numpy as jnp
from jax import lax
from jax.experimental import pallas as pl
from jax.experimental.pallas import tpu as pltpu
from jax.sharding import PartitionSpec as P

EPSILON = 1e-06
THETA = 1000000.0


def head_norm(value_rows, gain):
    mean_square = jnp.mean(value_rows * value_rows, axis=-1, keepdims=True)
    return value_rows * lax.rsqrt(mean_square + EPSILON) * gain


def rotate(value_rows, positions):
    width = value_rows.shape[-1]
    half = width // 2
    steps = jnp.arange(half).astype(jnp.float32)
    freqs = jnp.exp(steps * (-2.0 * math.log(THETA) / width))
    angles = positions[..., None] * freqs
    cosines = jnp.cos(angles)
    sines = jnp.sin(angles)
    first_part = value_rows[..., :half]
    second_part = value_rows[..., half:]
    return jnp.concatenate(
        [first_part * cosines - second_part * sines, second_part * cosines + first_part * sines],
        axis=-1,
    )


def attend_block(query, new_key_value, cached_key_rows, cached_value_rows, lengths, q_gain, k_gain):
    head = q_gain.shape[0]
    count = query.shape[0]
    kv_heads = new_key_value.shape[2] // head
    group = query.shape[1] // head // kv_heads
    slots = cached_key_rows.shape[1]
    positions = lengths.astype(jnp.float32)
    queries = query.astype(jnp.float32).reshape(count, kv_heads, group, head)
    queries = rotate(head_norm(queries, q_gain), positions[:, None, None]).astype(jnp.bfloat16)
    new_key = new_key_value[:, 0].astype(jnp.float32).reshape(count, kv_heads, head)
    new_key = rotate(head_norm(new_key, k_gain), positions[:, None]).astype(jnp.bfloat16)
    new_value = new_key_value[:, 1].reshape(count, kv_heads, head)
    stored_keys = cached_key_rows.reshape(count, slots, kv_heads, head)
    stored_values = cached_value_rows.reshape(count, slots, kv_heads, head)
    scale = 1.0 / math.sqrt(head)
    scores = (
        jnp.einsum("tkgd,tckd->tkgc", queries, stored_keys, preferred_element_type=jnp.float32)
        * scale
    )
    own_score = (
        jnp.einsum("tkgd,tkd->tkg", queries, new_key, preferred_element_type=jnp.float32) * scale
    )
    live = (jnp.arange(slots)[None, :] < lengths[:, None])[:, None, None, :]
    scores = jnp.where(live, scores, -jnp.inf)
    highest = jnp.maximum(jnp.max(scores, axis=-1), own_score)
    expos = jnp.where(live, jnp.exp(scores - highest[..., None]), 0.0)
    own_expo = jnp.exp(own_score - highest)
    total = jnp.sum(expos, axis=-1) + own_expo
    probs = (expos / total[..., None]).astype(jnp.bfloat16)
    own_prob = (own_expo / total).astype(jnp.bfloat16)
    summed = jnp.einsum("tkgc,tckd->tkgd", probs, stored_values, preferred_element_type=jnp.float32)
    summed = (
        summed
        + own_prob.astype(jnp.float32)[..., None] * new_value.astype(jnp.float32)[:, :, None, :]
    )
    return summed.astype(jnp.bfloat16).reshape(count, kv_heads * group * head)


MESH = pl.DeviceIdType.MESH
SIDE = 4
CHUNKS = 4


def place():
    y = lax.axis_index("dp")
    e = lax.axis_index("ep")
    return (e // 2) % SIDE, y, e // (2 * SIDE), e % 2


def device(x, y, z, core):
    return (y, (z * SIDE + x) * 2 + core)


def signal(target):
    pl.semaphore_signal(
        pltpu.get_barrier_semaphore(), inc=1, device_id=target, device_id_type=MESH
    )


def send(source, target, send_sem, recv_sem, where):
    pltpu.make_async_remote_copy(
        src_ref=source,
        dst_ref=target,
        send_sem=send_sem,
        recv_sem=recv_sem,
        device_id=where,
        device_id_type=MESH,
    ).start()


def wait(ref, sem):
    pltpu.make_async_copy(ref, ref, sem).wait()


def loop(first, last, body):
    def step(i, carry):
        body(i)
        return carry

    lax.fori_loop(first, last, step, 0)


def near_first(i):
    return 1 + 2 * i - 3 * (i // 2)


def project_kernel(
    heads, residual, weight, gain, attended, normed, columns, blocks, products, projected,
    weight_sems, first_send, first_recv, second_send, second_recv, back_send, back_recv,
):
    x, y, z, core = place()
    first = x * (1 - core) + z * core
    second = z * (1 - core) + x * core

    def at(f, s):
        return device(f * (1 - core) + s * core, y, s * (1 - core) + f * core, core)

    sibling = device(x, y, z, 1 - core)
    signal(sibling)

    def greet(i):
        other = (second * SIDE + first + i) % (SIDE * SIDE)
        signal(at(other % SIDE, other // SIDE))

    loop(1, SIDE * SIDE, greet)
    half = pl.ds(pl.multiple_of(core * 128, 128), 128)
    own_weight = pltpu.make_async_copy(weight, columns.at[:, half], weight_sems.at[0])
    own_weight.start()
    blocks[second, first] = heads[...]
    pl.semaphore_wait(pltpu.get_barrier_semaphore(), SIDE * SIDE)

    def start_first(i):
        f = (first + near_first(i)) % SIDE
        send(heads, blocks.at[second, first], first_send.at[f], first_recv.at[first], at(f, second))

    loop(0, SIDE - 1, start_first)

    def start_second(f):
        def one(i):
            s = (second + near_first(i)) % SIDE
            send(
                blocks.at[second, f], blocks.at[second, f], second_send.at[s, f],
                second_recv.at[second, f], at(first, s),
            )

        loop(0, SIDE - 1, one)

    start_second(first)
    send(weight, columns.at[:, half], weight_sems.at[1], weight_sems.at[2], sibling)

    def pass_on(i):
        f = (first + near_first(i)) % SIDE
        wait(blocks.at[second, f], first_recv.at[f])
        start_second(f)

    loop(0, SIDE - 1, pass_on)
    own_weight.wait()
    wait(weight, weight_sems.at[2])
    mine = pl.ds(pl.multiple_of((z * SIDE + x) * 256, 256), 256)

    def group(s):
        rows = blocks[s].reshape(SIDE * 16, blocks.shape[3])
        result = jnp.dot(rows, columns[...], preferred_element_type=jnp.float32)
        products[s] = result.astype(jnp.bfloat16).reshape(SIDE, 16, 256)

    def back(f, s):
        send(
            products.at[s, f], projected.at[:, mine], back_send.at[s, f],
            back_recv.at[second, first], at(f, s),
        )

    group(second)
    projected[:, mine] = products[second, first]
    loop(0, SIDE - 1, lambda i: back((first + near_first(i)) % SIDE, second))

    def other_group(i):
        s = (second + near_first(i)) % SIDE
        loop(0, SIDE, lambda f: wait(blocks.at[s, f], second_recv.at[s, f]))
        group(s)
        loop(0, SIDE, lambda f: back(f, s))

    loop(0, SIDE - 1, other_group)

    def collect(i):
        other = (second * SIDE + first + i) % (SIDE * SIDE)
        f, s = other % SIDE, other // SIDE
        wait(products.at[s, f], back_recv.at[s, f])

    loop(1, SIDE * SIDE, collect)
    total = residual[...].astype(jnp.float32) + projected[...].astype(jnp.float32)
    rounded = total.astype(jnp.bfloat16)
    attended[...] = rounded
    stream = rounded.astype(jnp.float32)
    level = lax.rsqrt(jnp.mean(stream * stream, axis=-1, keepdims=True) + EPSILON)
    normed[...] = (stream * level * gain[...]).astype(jnp.bfloat16)

    wait(weight, weight_sems.at[1])

    def finish_first(i):
        f = (first + 1 + i) % SIDE
        wait(heads, first_send.at[f])

        def finish_second(g):
            s = (second + 1 + i) % SIDE
            wait(blocks.at[second, g], second_send.at[s, g])

        loop(0, SIDE, finish_second)

    loop(0, SIDE - 1, finish_first)

    def finish_back(i):
        other = (second * SIDE + first + i) % (SIDE * SIDE)
        f, s = other % SIDE, other // SIDE
        wait(products.at[s, f], back_send.at[s, f])

    loop(1, SIDE * SIDE, finish_back)


def project(heads, residual, weight, gain):
    rows, width = heads.shape
    vmem = pl.BlockSpec(memory_space=pltpu.VMEM)
    sems = pltpu.SemaphoreType.DMA
    return pl.pallas_call(
        project_kernel,
        out_shape=[jax.ShapeDtypeStruct((rows, width), jnp.bfloat16)] * 2,
        in_specs=[vmem, vmem, pl.BlockSpec(memory_space=pl.ANY), vmem],
        out_specs=[vmem, vmem],
        scratch_shapes=[
            pltpu.VMEM((width, 256), jnp.bfloat16),
            pltpu.VMEM((SIDE, SIDE, rows, width), jnp.bfloat16),
            pltpu.VMEM((SIDE, SIDE, rows, 256), jnp.bfloat16),
            pltpu.VMEM((rows, width), jnp.bfloat16),
            sems((3,)),
            sems((SIDE,)),
            sems((SIDE,)),
            sems((SIDE, SIDE)),
            sems((SIDE, SIDE)),
            sems((SIDE, SIDE)),
            sems((SIDE, SIDE)),
        ],
        compiler_params=pltpu.CompilerParams(
            collective_id=1, has_side_effects=True, vmem_limit_bytes=24 << 20
        ),
        name="project",
    )(heads, residual, weight, gain)


def route(ids, probs):
    count, top = ids.shape
    experts = 128
    weights = probs / jnp.sum(probs, axis=-1, keepdims=True)
    label = lax.broadcasted_iota(jnp.int32, (count, experts), 1)
    named = jnp.zeros((count, experts), jnp.float32)
    value = jnp.zeros((count, experts), jnp.float32)
    for k in range(top):
        match = ids[:, k : k + 1] == label
        named = named + jnp.where(match, 1.0, 0.0)
        value = value + jnp.where(match, weights[:, k : k + 1], 0.0)
    below = lax.broadcasted_iota(jnp.int32, (count, count), 1) < lax.broadcasted_iota(
        jnp.int32, (count, count), 0
    )
    earlier = jnp.dot(
        jnp.where(below, 1.0, 0.0), named, preferred_element_type=jnp.float32
    )
    again = earlier > 0.5
    return jnp.concatenate(
        [jnp.where(again, 0.0, value), jnp.where(again, value, 0.0)], axis=1
    ).astype(jnp.bfloat16)


def experts_kernel(
    normed, attended, ids, probs, gate_up, down, mixed,
    gate_up_held, down_held, meta, rows_held, picked, received, total, answers, returned,
    partial, landed, summed, landed_last, choose, weigh,
    weight_sems, meta_sems, a_send, a_recv, b_send, b_recv, out_send, out_recv,
    ret_send, ret_recv, c_send, c_recv, d_send, d_recv,
):
    x, y, z, core = place()
    first = x * (1 - core) + z * core
    line = z * (1 - core) + x * core
    width = normed.shape[1]
    size = width // CHUNKS
    last = CHUNKS - 1

    def at(f, row, l, c):
        return device(f * (1 - core) + l * core, row, l * (1 - core) + f * core, c)

    def peer_first(f):
        return at(f, y, line, core)

    def peer_row(row):
        return at(first, row, line, core)

    def expert_at(e):
        return at(first, y, e // 2, e % 2)

    def source_at(q):
        c = q // SIDE
        l = q % SIDE
        return device(x * (1 - c) + l * c, y, l * (1 - c) + z * c, c)

    own_expert = line * 2 + core
    own_source = core * SIDE + line
    def answer_slot(q):
        c = q // SIDE
        return (z * (1 - c) + x * c) * 2 + core

    def cols(j):
        return pl.ds(pl.multiple_of(j * size, size), size)

    def others(body):
        loop(0, SIDE - 1, lambda i: body(near_first(i)))

    others(lambda d: signal(peer_first((first + d) % SIDE)))
    others(lambda d: signal(peer_row((y + d) % SIDE)))
    loop(1, 2 * SIDE, lambda i: signal(expert_at((own_expert + i) % (2 * SIDE))))
    loop(1, 2 * SIDE, lambda i: signal(source_at((own_source + i) % (2 * SIDE))))

    def fetch_gate_up(j):
        part = pl.ds(pl.multiple_of(j * size, size), size)
        return pltpu.make_async_copy(
            gate_up.at[0, part], gate_up_held.at[part], weight_sems.at[j]
        )

    def fetch_down(j):
        return pltpu.make_async_copy(
            down.at[0, :, cols(j)], down_held.at[:, cols(j)], weight_sems.at[CHUNKS + j]
        )

    loop(0, CHUNKS, lambda j: fetch_gate_up(j).start())
    loop(0, CHUNKS, lambda j: fetch_down(j).start())
    meta[y, first] = route(ids[...], probs[...])
    rows_held[y, first] = normed[...]
    pl.semaphore_wait(pltpu.get_barrier_semaphore(), 2 * (SIDE - 1) + 2 * (2 * SIDE - 1))

    def to_first(ref, slot, send_sem, recv_sem):
        def one(d):
            f = (first + d) % SIDE
            send(ref, slot, send_sem.at[f], recv_sem.at[first], peer_first(f))

        others(one)

    def to_rows(ref, slot, send_sem, recv_sem):
        def one(d):
            row = (y + d) % SIDE
            send(ref, slot, send_sem.at[row], recv_sem.at[y], peer_row(row))

        others(one)

    def wait_others(ref, own, sem):
        others(lambda d: wait(ref, sem.at[(own + d) % SIDE]))

    to_first(meta.at[y, first], meta.at[y, first], meta_sems.at[0], meta_sems.at[1])
    to_rows(
        normed.at[:, cols(last)], rows_held.at[y, first, :, cols(last)],
        a_send.at[last], a_recv.at[last],
    )

    def start_a(j):
        to_first(
            normed.at[:, cols(j)], rows_held.at[y, first, :, cols(j)], a_send.at[j], a_recv.at[j]
        )

    loop(0, last, start_a)
    wait_others(meta.at[y, first], first, meta_sems.at[1])
    to_rows(meta.at[y], meta.at[y], meta_sems.at[2], meta_sems.at[3])

    def start_b(j):
        wait_others(normed.at[:, cols(j)], first, a_recv.at[j])
        to_rows(
            rows_held.at[y, :, :, cols(j)], rows_held.at[y, :, :, cols(j)],
            b_send.at[j], b_recv.at[j],
        )

    start_b(0)
    wait_others(normed.at[:, cols(last)], y, a_recv.at[last])
    to_first(
        rows_held.at[:, first, :, cols(last)], rows_held.at[:, first, :, cols(last)],
        b_send.at[last], b_recv.at[last],
    )
    loop(1, last, start_b)

    wait_others(meta.at[y], y, meta_sems.at[3])
    tokens = SIDE * SIDE * 16
    known = meta[...].reshape(tokens, 256)
    row = lax.broadcasted_iota(jnp.int32, (tokens, 256), 0)
    lane = lax.broadcasted_iota(jnp.int32, (tokens, 256), 1)
    slot = row % 2
    expert = row // 32
    expert_x = x * (1 - core) + (expert // 2) * core
    expert_z = (expert // 2) * (1 - core) + z * core
    number = y * 32 + (expert_z * SIDE + expert_x) * 2 + expert % 2
    wanted = jnp.where(lane == slot * 128 + number, 1.0, 0.0).astype(jnp.bfloat16)
    nt = (((1,), (1,)), ((), ()))
    same = (row // 2) % 16 == lane // 16
    present = jnp.where(known.astype(jnp.float32) > 0.0, 1.0, 0.0).astype(jnp.bfloat16)
    chosen = lax.dot_general(wanted, present, nt, preferred_element_type=jnp.float32)
    choose[...] = jnp.where(same, chosen, 0.0).astype(jnp.bfloat16)
    same_back = row // 16 == (lane // 2) % 16
    scaled = lax.dot_general(known, wanted, nt, preferred_element_type=jnp.float32)
    weigh[...] = jnp.where(same_back, scaled, 0.0).astype(jnp.bfloat16)

    def pick(j):
        plane = rows_held[:, :, :, cols(j)].reshape(tokens, size)
        result = jnp.dot(choose[...], plane, preferred_element_type=jnp.float32)
        picked[:, :, cols(j)] = result.astype(jnp.bfloat16).reshape(2 * SIDE, 32, size)

        def one(i):
            e = (own_expert + i) % (2 * SIDE)
            send(
                picked.at[e, :, cols(j)], received.at[own_source, :, cols(j)],
                out_send.at[j, e], out_recv.at[j, own_source], expert_at(e),
            )

        loop(1, 2 * SIDE, one)
        received[own_source, :, cols(j)] = picked[own_expert, :, cols(j)]

    wait_others(rows_held.at[:, first, :, cols(last)], first, b_recv.at[last])
    pick(last)

    def finish_b(j):
        wait_others(rows_held.at[y, :, :, cols(j)], y, b_recv.at[j])
        pick(j)

    loop(0, last, finish_b)

    hidden_size = down.shape[1]

    def expand(i):
        j = (last + i) % CHUNKS

        def arrived(k):
            q = (own_source + k) % (2 * SIDE)
            wait(received.at[q, :, cols(j)], out_recv.at[j, q])

        loop(1, 2 * SIDE, arrived)
        fetch_gate_up(j).wait()
        part = pl.ds(pl.multiple_of(j * size, size), size)
        rows = received[:, :, cols(j)].reshape(tokens, size)

        def columns(n):
            piece = pl.ds(pl.multiple_of(n * 512, 512), 512)
            product = jnp.dot(rows, gate_up_held[part, piece], preferred_element_type=jnp.float32)

            @pl.when(i == 0)
            def _():
                total[:, piece] = product

            @pl.when(i > 0)
            def _():
                total[:, piece] += product

        loop(0, 2 * hidden_size // 512, columns)

    loop(0, CHUNKS, expand)
    gate = total[:, :hidden_size]
    hidden = (gate / (1.0 + jnp.exp(-gate)) * total[:, hidden_size:]).astype(jnp.bfloat16)

    def answer(j):
        fetch_down(j).wait()
        result = jnp.dot(hidden, down_held[:, cols(j)], preferred_element_type=jnp.float32)
        answers[:, :, cols(j)] = result.astype(jnp.bfloat16).reshape(2 * SIDE, 32, size)

        def one(i):
            q = (own_source + i) % (2 * SIDE)
            send(
                answers.at[q, :, cols(j)], returned.at[answer_slot(q), :, cols(j)],
                ret_send.at[j, q], ret_recv.at[j, answer_slot(q)], source_at(q),
            )

        loop(1, 2 * SIDE, one)
        returned[own_expert, :, cols(j)] = answers[own_source, :, cols(j)]

    loop(0, CHUNKS, answer)

    def combine(j):
        def arrived(k):
            e = (own_expert + k) % (2 * SIDE)
            wait(returned.at[e, :, cols(j)], ret_recv.at[j, e])

        loop(1, 2 * SIDE, arrived)
        rows = returned[:, :, cols(j)].reshape(tokens, size)
        result = jnp.dot(weigh[...], rows, preferred_element_type=jnp.float32)
        partial[:, :, :, cols(j)] = result.astype(jnp.bfloat16).reshape(SIDE, SIDE, 16, size)

    def combine_rows(j):
        combine(j)

        def one(d):
            r = (y + d) % SIDE
            send(
                partial.at[r, :, :, cols(j)], landed.at[y, :, :, cols(j)],
                c_send.at[j, r], c_recv.at[j, y], peer_row(r),
            )

        others(one)

    loop(0, last, combine_rows)
    combine(last)

    def one_last(d):
        f = (first + d) % SIDE
        send(
            partial.at[:, f, :, cols(last)], landed.at[first, :, :, cols(last)],
            c_send.at[last, f], c_recv.at[last, first], peer_first(f),
        )

    others(one_last)

    def add_up(own, j, index):
        block = own.astype(jnp.float32)
        for d in range(1, SIDE):
            block = block + landed[(index + d) % SIDE, :, :, cols(j)].astype(jnp.float32)
        summed[:, :, cols(j)] = block.astype(jnp.bfloat16)

    def gather_rows(j):
        wait_others(landed.at[0, :, :, cols(j)], y, c_recv.at[j])
        add_up(partial[y, :, :, cols(j)], j, y)

        def one(d):
            f = (first + d) % SIDE
            send(
                summed.at[f, :, cols(j)], landed_last.at[first, :, cols(j)],
                d_send.at[j, f], d_recv.at[j, first], peer_first(f),
            )

        others(one)

    loop(0, last, gather_rows)
    wait_others(landed.at[0, :, :, cols(last)], first, c_recv.at[last])
    add_up(partial[:, first, :, cols(last)], last, first)

    def one_row(d):
        r = (y + d) % SIDE
        send(
            summed.at[r, :, cols(last)], landed_last.at[y, :, cols(last)],
            d_send.at[last, r], d_recv.at[last, y], peer_row(r),
        )

    others(one_row)

    def finish(j, index):
        wait_others(landed_last.at[0, :, cols(j)], index, d_recv.at[j])
        block = summed[index, :, cols(j)].astype(jnp.float32)
        for d in range(1, SIDE):
            block = block + landed_last[(index + d) % SIDE, :, cols(j)].astype(jnp.float32)
        mixed[:, cols(j)] = (attended[:, cols(j)].astype(jnp.float32) + block).astype(jnp.bfloat16)

    loop(0, last, lambda j: finish(j, first))
    finish(last, y)

    def sent(j, index, other):
        wait_others(normed.at[:, cols(j)], index, a_send.at[j])
        wait_others(rows_held.at[0, :, :, cols(j)], other, b_send.at[j])
        wait_others(partial.at[0, :, :, cols(j)], other, c_send.at[j])
        wait_others(summed.at[0, :, cols(j)], index, d_send.at[j])

        def one(i):
            wait(picked.at[0, :, cols(j)], out_send.at[j, (own_expert + i) % (2 * SIDE)])
            wait(answers.at[0, :, cols(j)], ret_send.at[j, (own_source + i) % (2 * SIDE)])

        loop(1, 2 * SIDE, one)

    loop(0, last, lambda j: sent(j, first, y))
    sent(last, y, first)
    wait_others(meta.at[y, first], first, meta_sems.at[0])
    wait_others(meta.at[y], y, meta_sems.at[2])


def mix(normed, attended, ids, probs, gate_up, down):
    rows, width = normed.shape
    hidden = down.shape[1]
    tokens = SIDE * SIDE * rows
    vmem = pl.BlockSpec(memory_space=pltpu.VMEM)
    hbm = pl.BlockSpec(memory_space=pl.ANY)
    sems = pltpu.SemaphoreType.DMA
    bf16 = jnp.bfloat16
    return pl.pallas_call(
        experts_kernel,
        out_shape=jax.ShapeDtypeStruct((rows, width), bf16),
        in_specs=[vmem, vmem, vmem, vmem, hbm, hbm],
        out_specs=vmem,
        scratch_shapes=[
            pltpu.VMEM((width, 2 * hidden), bf16),
            pltpu.VMEM((hidden, width), bf16),
            pltpu.VMEM((SIDE, SIDE, rows, 256), bf16),
            pltpu.VMEM((SIDE, SIDE, rows, width), bf16),
            pltpu.VMEM((2 * SIDE, 32, width), bf16),
            pltpu.VMEM((2 * SIDE, 32, width), bf16),
            pltpu.VMEM((tokens, 2 * hidden), jnp.float32),
            pltpu.VMEM((2 * SIDE, 32, width), bf16),
            pltpu.VMEM((2 * SIDE, 32, width), bf16),
            pltpu.VMEM((SIDE, SIDE, rows, width), bf16),
            pltpu.VMEM((SIDE, SIDE, rows, width), bf16),
            pltpu.VMEM((SIDE, rows, width), bf16),
            pltpu.VMEM((SIDE, rows, width), bf16),
            pltpu.VMEM((tokens, tokens), bf16),
            pltpu.VMEM((tokens, tokens), bf16),
            sems((2 * CHUNKS,)),
            sems((4, SIDE)),
            sems((CHUNKS, SIDE)),
            sems((CHUNKS, SIDE)),
            sems((CHUNKS, SIDE)),
            sems((CHUNKS, SIDE)),
            sems((CHUNKS, 2 * SIDE)),
            sems((CHUNKS, 2 * SIDE)),
            sems((CHUNKS, 2 * SIDE)),
            sems((CHUNKS, 2 * SIDE)),
            sems((CHUNKS, SIDE)),
            sems((CHUNKS, SIDE)),
            sems((CHUNKS, SIDE)),
            sems((CHUNKS, SIDE)),
        ],
        compiler_params=pltpu.CompilerParams(
            collective_id=2, has_side_effects=True, vmem_limit_bytes=58 << 20
        ),
        name="experts",
    )(normed, attended, ids, probs, gate_up, down)


def local(
    residual,
    query,
    new_key_value,
    cached_key_rows,
    cached_value_rows,
    lengths,
    q_gain,
    k_gain,
    out_weight,
    moe_gain,
    expert_ids,
    gate_probs,
    expert_gate_up,
    expert_down,
):
    head_list = attend_block(
        query, new_key_value, cached_key_rows, cached_value_rows, lengths, q_gain, k_gain
    )
    attended, normed = project(head_list, residual, out_weight, moe_gain.reshape(1, -1))
    mixed = mix(normed, attended, expert_ids, gate_probs, expert_gate_up, expert_down)
    return (attended, mixed)


def solution(mesh):
    return jax.shard_map(
        local,
        mesh=mesh,
        in_specs=(
            P(("dp", "ep"), None),
            P(("dp", "ep"), None),
            P(("dp", "ep"), None, None),
            P(("dp", "ep"), None, None),
            P(("dp", "ep"), None, None),
            P(("dp", "ep")),
            P(),
            P(),
            P(None, "ep"),
            P(),
            P(("dp", "ep"), None),
            P(("dp", "ep"), None),
            P(("dp", "ep"), None, None),
            P(("dp", "ep"), None, None),
        ),
        out_specs=(P(("dp", "ep"), None), P(("dp", "ep"), None)),
        check_vma=False,
    )
```

```python
import math

import jax
import jax.numpy as jnp
from jax import lax
from jax.experimental import pallas as pl
from jax.experimental.pallas import tpu as pltpu
from jax.sharding import PartitionSpec as P

EPSILON = 1e-06
THETA = 1000000.0


MESH = pl.DeviceIdType.MESH
SIDE = 4
PLANE = 2 * SIDE * SIDE
GROUPS = ((0, 1280), (1280, 1536), (2816, 1280))
PARTS = (((0, 384), (0, 384), (0, 384)), ((384, 256), (384, 384), (384, 256)))


def place():
    y = lax.axis_index("dp")
    e = lax.axis_index("ep")
    return (e // 2) % SIDE, y, e // (2 * SIDE), e % 2


def device(x, y, z, core):
    return (y, (z * SIDE + x) * 2 + core)


def signal(target):
    pl.semaphore_signal(
        pltpu.get_barrier_semaphore(), inc=1, device_id=target, device_id_type=MESH
    )


def send(source, target, send_sem, recv_sem, where):
    pltpu.make_async_remote_copy(
        src_ref=source,
        dst_ref=target,
        send_sem=send_sem,
        recv_sem=recv_sem,
        device_id=where,
        device_id_type=MESH,
    ).start()


def wait(ref, sem):
    pltpu.make_async_copy(ref, ref, sem).wait()


def loop(first, last, body):
    def step(i, carry):
        body(i)
        return carry

    lax.fori_loop(first, last, step, 0)


def near_first(i):
    return 1 + 2 * i - 3 * (i // 2)


def route(ids, probs):
    top, count = ids.shape
    experts = 128
    weights = probs / jnp.sum(probs, axis=0, keepdims=True)
    label = iota((experts, count), 0)
    named = jnp.zeros((experts, count), jnp.float32)
    value = jnp.zeros((experts, count), jnp.float32)
    for k in range(top):
        match = ids[k : k + 1] == label
        named = named + jnp.where(match, 1.0, 0.0)
        value = value + jnp.where(match, weights[k : k + 1], 0.0)
    before = jnp.where(iota((count, count), 0) < iota((count, count), 1), 1.0, 0.0)
    earlier = jnp.dot(named, before, preferred_element_type=jnp.float32)
    again = earlier > 0.5
    both = jnp.concatenate(
        [jnp.where(again, 0.0, value), jnp.where(again, value, 0.0)], axis=0
    )
    return both.T.astype(jnp.bfloat16)


def turned(rows, cosines, sines, gain):
    mean_square = jnp.mean(rows * rows, axis=-1, keepdims=True)
    scaled = rows * lax.rsqrt(mean_square + EPSILON) * gain
    return (scaled * cosines + pltpu.roll(scaled, 64, 1) * sines).astype(jnp.bfloat16)


def halves(rows):
    width = rows.shape[1] // 2
    parts = rows.reshape(PLANE, 8, 2 * width)
    return jnp.concatenate([parts[:, :, :width], parts[:, :, width:]], axis=1).astype(jnp.bfloat16)


def iota(shape, dim):
    return lax.broadcasted_iota(jnp.int32, shape, dim)


def shifted(value, by, size):
    return (value >> by) & (size - 1)


def spot(axis, a, b, f):
    return ((f, a, b), (b, f, a), (b, a, f))[axis]


def ordered(axis, p, f, slot):
    x, y, z = spot(axis, shifted(p, 3, SIDE), shifted(p, 1, SIDE), f)
    return ((y * SIDE + z) * SIDE + x) * 4 + (p & 1) * 2 + slot


def ones_where(condition):
    return jnp.where(condition, 1.0, 0.0).astype(jnp.bfloat16)


def kernel(
    residual_in, query_in, new_in, keys_in, values_in, lengths, q_gain, k_gain, weight, moe_gain, ids, probs,
    gate_up, down, attended, mixed,
    query, keys, values, residual, scores, products_pv, heads, columns_held, blocks, products, projected,
    normed, gate_up_held, down_held, meta, shared, picked, received, total, answers, returned,
    partial, landed, choose, weigh, gather, spread,
    cache_sems, head_weight_sems, first_send, first_recv, second_send, second_recv, back_send, back_recv,
    weight_sems, meta_send, meta_recv, share_send, share_recv, out_send, out_recv,
    ret_send, ret_recv, sum_send, sum_recv,
):
    x, y, z, core = place()
    along = (x, y, z)
    across = ((y, z), (z, x), (y, x))
    axes = range(3)
    index = [(a * SIDE + b) * 2 + core for a, b in across]

    def on_line(axis, f):
        return device(*[f if i == axis else along[i] for i in axes], core)

    def in_plane(axis, p):
        return device(*spot(axis, p // (2 * SIDE), (p // 2) % SIDE, along[axis]), p % 2)

    def partner(axis, i):
        step = (13 * i) % PLANE
        a, b = across[axis]
        return (((a + step // (2 * SIDE)) % SIDE) * SIDE + (b + step // 2) % SIDE) * 2 + (core + step) % 2

    def each_partner(body):
        def one(i):
            for axis in axes:
                body(axis, partner(axis, i))

        loop(1, PLANE, one)

    def columns(axis):
        return pl.ds(*GROUPS[axis])

    def lanes(part, axis):
        start, size = PARTS[part][axis]
        return pl.ds(GROUPS[axis][0] // 2 + start, size)

    def both_columns(part, axis):
        start, size = PARTS[part][axis]
        base, width = GROUPS[axis]
        return pl.ds(base + start, size), pl.ds(base + width // 2 + start, size)

    loads = [
        pltpu.make_async_copy(source, target, cache_sems.at[i])
        for i, (source, target) in enumerate(
            ((query_in, query), (keys_in, keys), (values_in, values), (residual_in, residual))
        )
    ]
    for load in loads:
        load.start()
    half = pl.ds(pl.multiple_of(core * 128, 128), 128)
    own_weight = pltpu.make_async_copy(weight, columns_held.at[:, half], head_weight_sems.at[0])
    own_weight.start()
    each_partner(lambda axis, p: signal(in_plane(axis, p)))
    rows_of = [pl.ds(*group) for group in GROUPS]
    fetches = [
        pltpu.make_async_copy(gate_up.at[0, rows], gate_up_held.at[rows], weight_sems.at[i])
        for i, rows in enumerate(rows_of)
    ] + [
        pltpu.make_async_copy(down.at[0, :, rows], down_held.at[:, rows], weight_sems.at[3 + i])
        for i, rows in enumerate(rows_of)
    ]
    for fetch in fetches:
        fetch.start()
    own_meta = route(ids[...], probs[...])
    for axis in axes:
        meta[axis, along[axis]] = own_meta

    tokens, slots, group = 16, keys.shape[1], 16
    pairs = tokens * group
    nt = (((1,), (1,)), ((), ()))

    def exact(left, right, dims=(((1,), (0,)), ((), ()))):
        return lax.dot_general(left, right, dims, preferred_element_type=jnp.float32)

    count = jnp.broadcast_to(lengths[...].astype(jnp.float32), (128, tokens)).astype(jnp.bfloat16)
    same_token = ones_where(iota((pairs, tokens), 0) >> 4 == iota((pairs, tokens), 1))
    eye = ones_where(iota((tokens, tokens), 0) == iota((tokens, tokens), 1))
    position = exact(eye, count, nt)
    lane = iota((tokens, 128), 1)
    freqs = jnp.exp((lane & 63).astype(jnp.float32) * (-2.0 * math.log(THETA) / 128))
    angles = position * freqs
    cosines = jnp.cos(angles)
    sines = jnp.where(lane < 64, -1.0, 1.0) * jnp.sin(angles)
    row, col = iota((pairs, pairs), 0), iota((pairs, pairs), 1)
    swap = ones_where(((row >> 4) == (col & 15)) & ((row & 15) == (col >> 4)))
    live = iota((pairs, slots), 1) < jnp.concatenate(
        [exact(same_token, count, nt)] * (slots // 128), axis=1
    ).astype(jnp.int32)
    scale = 1.0 / math.sqrt(128)
    many_cosines = jnp.concatenate([cosines] * group, axis=0)
    many_sines = jnp.concatenate([sines] * group, axis=0)
    loads[0].wait()
    queries, own_scores = [], []
    for kv in range(2):
        stack = jnp.concatenate(
            [query[:, (kv * group + h) * 128 : (kv * group + h + 1) * 128] for h in range(group)], axis=0
        ).astype(jnp.float32)
        rotated = exact(swap, turned(stack, many_cosines, many_sines, q_gain[...]))
        new_key = turned(
            new_in[:, kv * 128 : kv * 128 + 128].astype(jnp.float32), cosines, sines, k_gain[...]
        )
        own = jnp.sum(rotated * exact(same_token, new_key), axis=-1, keepdims=True) * scale
        queries.append(rotated.astype(jnp.bfloat16))
        own_scores.append(own)
    loads[1].wait()
    for kv in range(2):
        lanes_of = slice(kv * 128, kv * 128 + 128)
        for t in range(tokens):
            scores[kv, t * group : (t + 1) * group] = exact(
                queries[kv][t * group : (t + 1) * group], keys[t, :, lanes_of], nt
            )
    loads[2].wait()

    def attend(kv):
        lanes_of = slice(kv * 128, kv * 128 + 128)
        own = own_scores[kv]
        masked = jnp.where(live, scores[kv] * scale, -jnp.inf)
        highest = jnp.maximum(jnp.max(masked, axis=-1, keepdims=True), own)
        expos = jnp.exp(masked - highest)
        own_expo = jnp.exp(own - highest)
        sums = jnp.sum(expos, axis=-1, keepdims=True) + own_expo
        probs_of = (expos / sums).astype(jnp.bfloat16)
        own_prob = (own_expo / sums).astype(jnp.bfloat16).astype(jnp.float32)
        for t in range(tokens):
            products_pv[t * group : (t + 1) * group] = exact(
                probs_of[t * group : (t + 1) * group], values[t, :, lanes_of]
            )
        new_value = exact(same_token, new_in[:, 256 + kv * 128 : 384 + kv * 128])
        result = (products_pv[...] + own_prob * new_value).astype(jnp.bfloat16)
        result = exact(swap, result).astype(jnp.bfloat16)
        for h in range(group):
            heads[:, (kv * group + h) * 128 : (kv * group + h + 1) * 128] = result[
                h * tokens : (h + 1) * tokens
            ]

    first = x * (1 - core) + z * core
    second = z * (1 - core) + x * core

    def at(f, s):
        return device(f * (1 - core) + s * core, y, s * (1 - core) + f * core, core)

    width = heads.shape[1]
    wide = width // 2

    def side(kv):
        return pl.ds(kv * wide, wide)

    def start_first(kv):
        def one(i):
            f = (first + near_first(i)) % SIDE
            send(
                heads.at[:, side(kv)], blocks.at[second, first, :, side(kv)],
                first_send.at[kv, f], first_recv.at[kv, first], at(f, second),
            )

        loop(0, SIDE - 1, one)

    def start_second(kv, f, source):
        def one(i):
            s = (second + near_first(i)) % SIDE
            send(
                source, blocks.at[second, f, :, side(kv)], second_send.at[kv, s, f],
                second_recv.at[kv, second, f], at(first, s),
            )

        loop(0, SIDE - 1, one)

    sibling = device(x, y, z, 1 - core)
    attend(0)
    pl.semaphore_wait(pltpu.get_barrier_semaphore(), 3 * (PLANE - 1))
    start_first(0)
    start_second(0, first, heads.at[:, side(0)])
    attend(1)
    start_first(1)
    start_second(1, first, heads.at[:, side(1)])
    send(weight, columns_held.at[:, half], head_weight_sems.at[1], head_weight_sems.at[2], sibling)

    def to_line(axis, body):
        def one(i):
            body((along[axis] + near_first(i)) % SIDE)

        loop(0, SIDE - 1, one)

    for axis in axes:
        own = along[axis]
        to_line(axis, lambda f: send(
            meta.at[axis, own], meta.at[axis, own], meta_send.at[axis, f], meta_recv.at[axis, own],
            on_line(axis, f),
        ))
    blocks[second, first] = heads[...]
    for kv in range(2):
        def pass_on(i):
            f = (first + near_first(i)) % SIDE
            wait(blocks.at[second, f, :, side(kv)], first_recv.at[kv, f])
            start_second(kv, f, blocks.at[second, f, :, side(kv)])

        loop(0, SIDE - 1, pass_on)
    own_weight.wait()
    wait(weight, head_weight_sems.at[2])
    mine = pl.ds(pl.multiple_of((z * SIDE + x) * 256, 256), 256)

    def project(s):
        rows = blocks[s].reshape(SIDE * tokens, width)
        products[s] = exact(rows, columns_held[...]).astype(jnp.bfloat16).reshape(SIDE, tokens, 256)

    def back(f, s):
        send(
            products.at[s, f], projected.at[:, mine], back_send.at[s, f],
            back_recv.at[second, first], at(f, s),
        )

    project(second)
    projected[:, mine] = products[second, first]
    loop(0, SIDE - 1, lambda i: back((first + near_first(i)) % SIDE, second))

    for axis in axes:
        q = iota((1, 512), 1)
        target = ordered(axis, q >> 4, shifted(q, 1, SIDE), q & 1) + shifted(q, 3, 2) * 256
        gather[axis] = ones_where(iota((512, 512), 0) == target)
        q = iota((256, 1), 0)
        target = ordered(axis, q >> 3, shifted(q, 1, SIDE), q & 1)
        spread[axis] = ones_where(iota((256, 256), 1) == target)

    for axis in axes:
        to_line(axis, lambda f: wait(meta.at[axis, 0], meta_recv.at[axis, f]))
        known = meta[axis].reshape(SIDE * 16, 256)
        present = ones_where(known.astype(jnp.float32) > 0.0)

        def expert(p):
            ex, ey, ez = spot(axis, shifted(p, 3, SIDE), shifted(p, 1, SIDE), along[axis])
            return (ey * SIDE + ez) * (2 * SIDE) + ex * 2 + (p & 1)

        q = iota((256, 1), 0)
        wanted = ones_where(iota((256, 256), 1) == (q & 1) * 128 + expert(q >> 3))
        chosen = lax.dot_general(wanted, present, nt, preferred_element_type=jnp.float32)
        same = shifted(q, 1, SIDE) == iota((1, SIDE * 16), 1) >> 4
        choose[axis] = jnp.where(same, chosen, 0.0).astype(jnp.bfloat16)
        q = iota((512, 1), 0)
        wanted = ones_where(iota((512, 256), 1) == (q & 1) * 128 + expert(q >> 4))
        scaled = lax.dot_general(known, wanted, nt, preferred_element_type=jnp.float32)
        q = iota((1, 512), 1)
        scaled = jnp.where(iota((SIDE * 16, 1), 0) >> 4 == shifted(q, 1, SIDE), scaled, 0.0)
        upper = shifted(q, 3, 2) == 0
        weigh[axis] = jnp.concatenate(
            [jnp.where(upper, scaled, 0.0), jnp.where(upper, 0.0, scaled)], axis=0
        ).astype(jnp.bfloat16)

    def other_group(i):
        s = (second + near_first(i)) % SIDE

        def arrived(f):
            for kv in range(2):
                wait(blocks.at[s, f, :, side(kv)], second_recv.at[kv, s, f])

        loop(0, SIDE, arrived)
        project(s)
        loop(0, SIDE, lambda f: back(f, s))

    loop(0, SIDE - 1, other_group)

    def others_in_plane(body):
        def one(i):
            other = (second * SIDE + first + i) % (SIDE * SIDE)
            body(other % SIDE, other // SIDE)

        loop(1, SIDE * SIDE, one)

    others_in_plane(lambda f, s: wait(products.at[s, f], back_recv.at[s, f]))
    loads[3].wait()
    added = residual[...].astype(jnp.float32) + projected[...].astype(jnp.float32)
    rounded = added.astype(jnp.bfloat16)
    attended[...] = rounded
    stream = rounded.astype(jnp.float32)
    level = lax.rsqrt(jnp.mean(stream * stream, axis=-1, keepdims=True) + EPSILON)
    normed[...] = (stream * level * moe_gain[...]).astype(jnp.bfloat16)
    for axis in axes:
        own = along[axis]
        to_line(axis, lambda f: send(
            normed.at[:, columns(axis)], shared.at[own, :, columns(axis)],
            share_send.at[axis, f], share_recv.at[axis, own], on_line(axis, f),
        ))
        shared[along[axis], :, columns(axis)] = normed[:, columns(axis)]

    for axis in axes:
        to_line(axis, lambda f: wait(shared.at[0, :, columns(axis)], share_recv.at[axis, f]))
        rows = shared[:, :, columns(axis)].reshape(SIDE * 16, GROUPS[axis][1])
        result = jnp.dot(choose[axis], rows, preferred_element_type=jnp.float32)
        base, width = GROUPS[axis]
        picked[:, :, pl.ds(base // 2, width // 2)] = halves(result)
    for part in range(len(PARTS)):
        each_partner(lambda axis, p: send(
            picked.at[p, :, lanes(part, axis)], received.at[index[axis], :, lanes(part, axis)],
            out_send.at[part, axis], out_recv.at[part, axis], in_plane(axis, p),
        ))
    for axis in axes:
        base, width = GROUPS[axis]
        whole = pl.ds(base // 2, width // 2)
        received[index[axis], :, whole] = picked[index[axis], :, whole]

    hidden_size = down.shape[1]
    many = pl.ds(0, PLANE - 1)
    for part in range(len(PARTS)):
        for axis in axes:
            wait(received.at[many, :, lanes(part, axis)], out_recv.at[part, axis])
            if part == 0:
                fetches[axis].wait()
            size = PARTS[part][axis][1]
            messages = received[:, :, lanes(part, axis)].reshape(PLANE * 16, size)
            rows = jnp.dot(gather[axis], messages, preferred_element_type=jnp.float32)
            rows = rows.astype(jnp.bfloat16)
            upper, lower = both_columns(part, axis)

            def step(n):
                piece = pl.ds(pl.multiple_of(n * 512, 512), 512)
                product = jnp.dot(
                    rows[:256], gate_up_held[upper, piece], preferred_element_type=jnp.float32
                ) + jnp.dot(
                    rows[256:], gate_up_held[lower, piece], preferred_element_type=jnp.float32
                )
                if part == 0 and axis == 0:
                    total[:, piece] = product
                else:
                    total[:, piece] += product

            loop(0, 2 * hidden_size // 512, step)

    gate = total[:, :hidden_size]
    hidden = (gate / (1.0 + jnp.exp(-gate)) * total[:, hidden_size:]).astype(jnp.bfloat16)
    for axis in axes:
        fetches[3 + axis].wait()
    hiddens = [
        jnp.dot(spread[axis], hidden, preferred_element_type=jnp.float32).astype(jnp.bfloat16)
        for axis in axes
    ]
    for part in range(len(PARTS)):
        for axis in axes:
            upper, lower = both_columns(part, axis)
            result = [
                jnp.dot(hiddens[axis], down_held[:, cols], preferred_element_type=jnp.float32)
                for cols in (upper, lower)
            ]
            answers[:, :, lanes(part, axis)] = halves(jnp.concatenate(result, axis=1))
        each_partner(lambda axis, p: send(
            answers.at[p, :, lanes(part, axis)], returned.at[index[axis], :, lanes(part, axis)],
            ret_send.at[part, axis], ret_recv.at[part, axis], in_plane(axis, p),
        ))
        for axis in axes:
            returned[index[axis], :, lanes(part, axis)] = answers[index[axis], :, lanes(part, axis)]

    for part in range(len(PARTS)):
        for axis in axes:
            wait(returned.at[many, :, lanes(part, axis)], ret_recv.at[part, axis])
            size = PARTS[part][axis][1]
            messages = returned[:, :, lanes(part, axis)].reshape(PLANE * 16, size)
            result = jnp.dot(weigh[axis], messages, preferred_element_type=jnp.float32)
            result = result.astype(jnp.bfloat16).reshape(2, SIDE, 16, size)
            upper, lower = both_columns(part, axis)
            partial[:, :, upper] = result[0]
            partial[:, :, lower] = result[1]
            if part == len(PARTS) - 1:
                own = along[axis]
                to_line(axis, lambda f: send(
                    partial.at[f, :, columns(axis)], landed.at[own, :, columns(axis)],
                    sum_send.at[axis, f], sum_recv.at[axis, own], on_line(axis, f),
                ))
    for axis in axes:
        to_line(axis, lambda f: wait(landed.at[0, :, columns(axis)], sum_recv.at[axis, f]))
        own = along[axis]
        block = partial[own, :, columns(axis)].astype(jnp.float32)
        for d in range(1, SIDE):
            block = block + landed[(own + d) % SIDE, :, columns(axis)].astype(jnp.float32)
        block = block + attended[:, columns(axis)].astype(jnp.float32)
        mixed[:, columns(axis)] = block.astype(jnp.bfloat16)

    wait(weight, head_weight_sems.at[1])
    for kv in range(2):
        def finish_first(i):
            f = (first + 1 + i) % SIDE
            s = (second + 1 + i) % SIDE
            wait(heads.at[:, side(kv)], first_send.at[kv, f])
            loop(0, SIDE, lambda g: wait(heads.at[:, side(kv)], second_send.at[kv, s, g]))

        loop(0, SIDE - 1, finish_first)
    others_in_plane(lambda f, s: wait(products.at[s, f], back_send.at[s, f]))
    for axis in axes:
        to_line(axis, lambda f: wait(meta.at[axis, 0], meta_send.at[axis, f]))
        to_line(axis, lambda f: wait(landed.at[0, :, columns(axis)], share_send.at[axis, f]))
        to_line(axis, lambda f: wait(landed.at[0, :, columns(axis)], sum_send.at[axis, f]))
        for part in range(len(PARTS)):
            wait(picked.at[many, :, lanes(part, axis)], out_send.at[part, axis])
            wait(answers.at[many, :, lanes(part, axis)], ret_send.at[part, axis])


def local(
    residual,
    query,
    new_key_value,
    cached_key_rows,
    cached_value_rows,
    lengths,
    q_gain,
    k_gain,
    out_weight,
    moe_gain,
    expert_ids,
    gate_probs,
    expert_gate_up,
    expert_down,
):
    rows, width = residual.shape
    hidden = expert_down.shape[1]
    slots = cached_key_rows.shape[1]
    vmem = pl.BlockSpec(memory_space=pltpu.VMEM)
    hbm = pl.BlockSpec(memory_space=pl.ANY)
    sems = pltpu.SemaphoreType.DMA
    bf16 = jnp.bfloat16
    own = pltpu.VMEM((rows, width), bf16)
    caches = pltpu.VMEM(cached_key_rows.shape, bf16)
    messages = pltpu.VMEM((PLANE, 16, width // 2), bf16)
    lines = pltpu.VMEM((SIDE, rows, width), bf16)
    parts = len(PARTS)
    attended, mixed = pl.pallas_call(
        kernel,
        out_shape=[jax.ShapeDtypeStruct((rows, width), bf16)] * 2,
        in_specs=[hbm, hbm, vmem, hbm, hbm, vmem, vmem, vmem, hbm, vmem, vmem, vmem, hbm, hbm],
        out_specs=[vmem, vmem],
        scratch_shapes=[
            own,
            caches,
            caches,
            own,
            pltpu.VMEM((2, 256, slots), jnp.float32),
            pltpu.VMEM((256, 128), jnp.float32),
            own,
            pltpu.VMEM((width, 256), bf16),
            pltpu.VMEM((SIDE, SIDE, rows, width), bf16),
            pltpu.VMEM((SIDE, SIDE, rows, 256), bf16),
            own,
            own,
            pltpu.VMEM((width, 2 * hidden), bf16),
            pltpu.VMEM((hidden, width), bf16),
            pltpu.VMEM((3, SIDE, rows, 256), bf16),
            lines,
            messages,
            messages,
            pltpu.VMEM((256, 2 * hidden), jnp.float32),
            messages,
            messages,
            lines,
            lines,
            pltpu.VMEM((3, 256, SIDE * rows), bf16),
            pltpu.VMEM((3, 2 * SIDE * rows, 512), bf16),
            pltpu.VMEM((3, 512, 512), bf16),
            pltpu.VMEM((3, 256, 256), bf16),
            sems((4,)),
            sems((3,)),
            sems((2, SIDE)),
            sems((2, SIDE)),
            sems((2, SIDE, SIDE)),
            sems((2, SIDE, SIDE)),
            sems((SIDE, SIDE)),
            sems((SIDE, SIDE)),
            sems((6,)),
            sems((3, SIDE)),
            sems((3, SIDE)),
            sems((3, SIDE)),
            sems((3, SIDE)),
            sems((parts, 3)),
            sems((parts, 3)),
            sems((parts, 3)),
            sems((parts, 3)),
            sems((3, SIDE)),
            sems((3, SIDE)),
        ],
        compiler_params=pltpu.CompilerParams(
            collective_id=1, has_side_effects=True, vmem_limit_bytes=60 << 20
        ),
        name="layer",
    )(
        residual, query, new_key_value.reshape(rows, 512), cached_key_rows, cached_value_rows,
        lengths.reshape(1, rows), q_gain.reshape(1, 128), k_gain.reshape(1, 128), out_weight,
        moe_gain.reshape(1, width), expert_ids.T, gate_probs.T, expert_gate_up, expert_down,
    )
    return (attended, mixed)


def solution(mesh):
    return jax.shard_map(
        local,
        mesh=mesh,
        in_specs=(
            P(("dp", "ep"), None),
            P(("dp", "ep"), None),
            P(("dp", "ep"), None, None),
            P(("dp", "ep"), None, None),
            P(("dp", "ep"), None, None),
            P(("dp", "ep")),
            P(),
            P(),
            P(None, "ep"),
            P(),
            P(("dp", "ep"), None),
            P(("dp", "ep"), None),
            P(("dp", "ep"), None, None),
            P(("dp", "ep"), None, None),
        ),
        out_specs=(P(("dp", "ep"), None), P(("dp", "ep"), None)),
        check_vma=False,
    )
```

```python
import math

import jax
import jax.numpy as jnp
from jax import lax
from jax.experimental import pallas as pl
from jax.experimental.pallas import tpu as pltpu
from jax.sharding import PartitionSpec as P

EPSILON = 1e-06
THETA = 1000000.0


MESH = pl.DeviceIdType.MESH
SIDE = 4
PLANE = 2 * SIDE * SIDE
GROUPS = ((0, 1280), (1280, 1536), (2816, 1280))
PARTS = (
    ((0, 256), (0, 256), (0, 256)),
    ((256, 256), (256, 256), (256, 256)),
    ((512, 128), (512, 256), (512, 128)),
)


def place():
    y = lax.axis_index("dp")
    e = lax.axis_index("ep")
    return (e // 2) % SIDE, y, e // (2 * SIDE), e % 2


def device(x, y, z, core):
    return (y, (z * SIDE + x) * 2 + core)


def signal(target):
    pl.semaphore_signal(
        pltpu.get_barrier_semaphore(), inc=1, device_id=target, device_id_type=MESH
    )


def send(source, target, send_sem, recv_sem, where):
    pltpu.make_async_remote_copy(
        src_ref=source,
        dst_ref=target,
        send_sem=send_sem,
        recv_sem=recv_sem,
        device_id=where,
        device_id_type=MESH,
    ).start()


def wait(ref, sem):
    pltpu.make_async_copy(ref, ref, sem).wait()


def loop(first, last, body):
    def step(i, carry):
        body(i)
        return carry

    lax.fori_loop(first, last, step, 0)


def near_first(i):
    return 1 + 2 * i - 3 * (i // 2)


def route(ids, probs):
    top, count = ids.shape
    experts = 128
    weights = probs / jnp.sum(probs, axis=0, keepdims=True)
    label = iota((experts, count), 0)
    named = jnp.zeros((experts, count), jnp.float32)
    value = jnp.zeros((experts, count), jnp.float32)
    for k in range(top):
        match = ids[k : k + 1] == label
        named = named + jnp.where(match, 1.0, 0.0)
        value = value + jnp.where(match, weights[k : k + 1], 0.0)
    before = jnp.where(iota((count, count), 0) < iota((count, count), 1), 1.0, 0.0)
    earlier = jnp.dot(named, before, preferred_element_type=jnp.float32)
    again = earlier > 0.5
    both = jnp.concatenate(
        [jnp.where(again, 0.0, value), jnp.where(again, value, 0.0)], axis=0
    )
    return both.T.astype(jnp.bfloat16)


def turned(rows, cosines, sines, gain):
    mean_square = jnp.mean(rows * rows, axis=-1, keepdims=True)
    scaled = rows * lax.rsqrt(mean_square + EPSILON) * gain
    return (scaled * cosines + pltpu.roll(scaled, 64, 1) * sines).astype(jnp.bfloat16)


def halves(rows):
    width = rows.shape[1] // 2
    parts = rows.reshape(PLANE, 8, 2 * width)
    return jnp.concatenate([parts[:, :, :width], parts[:, :, width:]], axis=1).astype(jnp.bfloat16)


def iota(shape, dim):
    return lax.broadcasted_iota(jnp.int32, shape, dim)


def shifted(value, by, size):
    return (value >> by) & (size - 1)


def spot(axis, a, b, f):
    return ((f, a, b), (b, f, a), (b, a, f))[axis]


def ordered(axis, p, f, slot):
    x, y, z = spot(axis, shifted(p, 3, SIDE), shifted(p, 1, SIDE), f)
    return ((y * SIDE + z) * SIDE + x) * 4 + (p & 1) * 2 + slot


def ones_where(condition):
    return jnp.where(condition, 1.0, 0.0).astype(jnp.bfloat16)


def kernel(
    residual_in, query_in, new_in, keys_in, values_in, lengths_in, q_gain_in, k_gain_in, weight, moe_gain_in,
    ids_in, probs_in, gate_up, down, out,
    query, keys, values, residual, new, lengths, q_gain, k_gain, moe_gain, ids, probs, scores, products_pv, heads, columns_held, blocks, products, projected,
    normed, gate_up_held, down_held, meta, shared, picked, received, total, answers, returned,
    partial, landed, choose, weigh, gather, spread,
    cache_sems, head_weight_sems, first_send, first_recv, second_send, second_recv, back_send, back_recv,
    weight_sems, meta_send, meta_recv, share_send, share_recv, out_send, out_recv,
    ret_send, ret_recv, sum_send, sum_recv,
):
    attended, mixed = out.at[0], out.at[1]
    x, y, z, core = place()
    along = (x, y, z)
    across = ((y, z), (z, x), (y, x))
    axes = range(3)
    index = [(a * SIDE + b) * 2 + core for a, b in across]

    def on_line(axis, f):
        return device(*[f if i == axis else along[i] for i in axes], core)

    def in_plane(axis, p):
        return device(*spot(axis, p // (2 * SIDE), (p // 2) % SIDE, along[axis]), p % 2)

    def partner(axis, i):
        step = (13 * i) % PLANE
        a, b = across[axis]
        return (((a + step // (2 * SIDE)) % SIDE) * SIDE + (b + step // 2) % SIDE) * 2 + (core + step) % 2

    def each_partner(body):
        def one(i):
            for axis in axes:
                body(axis, partner(axis, i))

        loop(1, PLANE, one)

    def columns(axis):
        return pl.ds(*GROUPS[axis])

    def lanes(part, axis):
        start, size = PARTS[part][axis]
        return pl.ds(GROUPS[axis][0] // 2 + start, size)

    def both_columns(part, axis):
        start, size = PARTS[part][axis]
        base, width = GROUPS[axis]
        return pl.ds(base + start, size), pl.ds(base + width // 2 + start, size)

    loads = [
        pltpu.make_async_copy(source, target, cache_sems.at[i])
        for i, (source, target) in enumerate(
            (
                (query_in, query), (keys_in, keys), (values_in, values), (residual_in, residual),
                (new_in, new), (lengths_in, lengths), (q_gain_in, q_gain), (k_gain_in, k_gain),
                (moe_gain_in, moe_gain), (ids_in, ids), (probs_in, probs),
            )
        )
    ]
    for load in loads:
        load.start()
    half = pl.ds(pl.multiple_of(core * 128, 128), 128)
    own_weight = pltpu.make_async_copy(weight, columns_held.at[:, half], head_weight_sems.at[0])
    own_weight.start()
    def greet(i):
        other = (z * SIDE + x + i) % (SIDE * SIDE)
        signal(device(other % SIDE, y, other // SIDE, core))

    def greet_row(i):
        row = (y + i) % SIDE
        signal(device(x, row, z, core))
        signal(device(x, row, z, 1 - core))

    signal(device(x, y, z, 1 - core))
    loop(1, SIDE * SIDE, greet)
    loop(1, SIDE, greet_row)
    rows_of = [pl.ds(*group) for group in GROUPS]
    fetches = [
        pltpu.make_async_copy(gate_up.at[0, rows], gate_up_held.at[rows], weight_sems.at[i])
        for i, rows in enumerate(rows_of)
    ] + [
        pltpu.make_async_copy(down.at[0, :, rows], down_held.at[:, rows], weight_sems.at[3 + i])
        for i, rows in enumerate(rows_of)
    ]
    for fetch in fetches:
        fetch.start()
    for load in loads[4:]:
        load.wait()
    own_meta = route(ids[...], probs[...])
    for axis in axes:
        meta[axis, along[axis]] = own_meta

    tokens, slots, group = 16, keys.shape[1], 16
    pairs = tokens * group
    nt = (((1,), (1,)), ((), ()))

    def exact(left, right, dims=(((1,), (0,)), ((), ()))):
        return lax.dot_general(left, right, dims, preferred_element_type=jnp.float32)

    count = jnp.broadcast_to(lengths[...].astype(jnp.float32), (128, tokens)).astype(jnp.bfloat16)
    same_token = ones_where(iota((pairs, tokens), 0) >> 4 == iota((pairs, tokens), 1))
    eye = ones_where(iota((tokens, tokens), 0) == iota((tokens, tokens), 1))
    position = exact(eye, count, nt)
    lane = iota((tokens, 128), 1)
    freqs = jnp.exp((lane & 63).astype(jnp.float32) * (-2.0 * math.log(THETA) / 128))
    angles = position * freqs
    cosines = jnp.cos(angles)
    sines = jnp.where(lane < 64, -1.0, 1.0) * jnp.sin(angles)
    row, col = iota((pairs, pairs), 0), iota((pairs, pairs), 1)
    swap = ones_where(((row >> 4) == (col & 15)) & ((row & 15) == (col >> 4)))
    live = iota((pairs, slots), 1) < jnp.concatenate(
        [exact(same_token, count, nt)] * (slots // 128), axis=1
    ).astype(jnp.int32)
    scale = 1.0 / math.sqrt(128)
    many_cosines = jnp.concatenate([cosines] * group, axis=0)
    many_sines = jnp.concatenate([sines] * group, axis=0)
    loads[0].wait()
    queries, own_scores = [], []
    for kv in range(2):
        stack = jnp.concatenate(
            [query[:, (kv * group + h) * 128 : (kv * group + h + 1) * 128] for h in range(group)], axis=0
        ).astype(jnp.float32)
        rotated = exact(swap, turned(stack, many_cosines, many_sines, q_gain[...]))
        new_key = turned(
            new[:, 0, kv * 128 : kv * 128 + 128].astype(jnp.float32), cosines, sines, k_gain[...]
        )
        own = jnp.sum(rotated * exact(same_token, new_key), axis=-1, keepdims=True) * scale
        queries.append(rotated.astype(jnp.bfloat16))
        own_scores.append(own)
    loads[1].wait()
    for kv in range(2):
        lanes_of = slice(kv * 128, kv * 128 + 128)
        for t in range(tokens):
            scores[kv, t * group : (t + 1) * group] = exact(
                queries[kv][t * group : (t + 1) * group], keys[t, :, lanes_of], nt
            )
    loads[2].wait()

    def attend(kv):
        lanes_of = slice(kv * 128, kv * 128 + 128)
        own = own_scores[kv]
        masked = jnp.where(live, scores[kv] * scale, -jnp.inf)
        highest = jnp.maximum(jnp.max(masked, axis=-1, keepdims=True), own)
        expos = jnp.exp(masked - highest)
        own_expo = jnp.exp(own - highest)
        sums = jnp.sum(expos, axis=-1, keepdims=True) + own_expo
        probs_of = (expos / sums).astype(jnp.bfloat16)
        own_prob = (own_expo / sums).astype(jnp.bfloat16).astype(jnp.float32)
        for t in range(tokens):
            products_pv[t * group : (t + 1) * group] = exact(
                probs_of[t * group : (t + 1) * group], values[t, :, lanes_of]
            )
        new_value = exact(same_token, new[:, 1, kv * 128 : kv * 128 + 128])
        result = (products_pv[...] + own_prob * new_value).astype(jnp.bfloat16)
        result = exact(swap, result).astype(jnp.bfloat16)
        for h in range(group):
            heads[:, (kv * group + h) * 128 : (kv * group + h + 1) * 128] = result[
                h * tokens : (h + 1) * tokens
            ]

    first = x * (1 - core) + z * core
    second = z * (1 - core) + x * core

    def at(f, s):
        return device(f * (1 - core) + s * core, y, s * (1 - core) + f * core, core)

    width = heads.shape[1]
    wide = width // 2

    def side(kv):
        return pl.ds(kv * wide, wide)

    def start_first(kv):
        def one(i):
            f = (first + near_first(i)) % SIDE
            send(
                heads.at[:, side(kv)], blocks.at[second, first, :, side(kv)],
                first_send.at[kv, f], first_recv.at[kv, first], at(f, second),
            )

        loop(0, SIDE - 1, one)

    def start_second(kv, f, source):
        def one(i):
            s = (second + near_first(i)) % SIDE
            send(
                source, blocks.at[second, f, :, side(kv)], second_send.at[kv, s, f],
                second_recv.at[kv, second, f], at(first, s),
            )

        loop(0, SIDE - 1, one)

    sibling = device(x, y, z, 1 - core)
    attend(0)
    pl.semaphore_wait(pltpu.get_barrier_semaphore(), SIDE * SIDE + 2 * (SIDE - 1))
    start_first(0)
    start_second(0, first, heads.at[:, side(0)])
    attend(1)
    start_first(1)
    start_second(1, first, heads.at[:, side(1)])
    send(weight, columns_held.at[:, half], head_weight_sems.at[1], head_weight_sems.at[2], sibling)

    def to_line(axis, body):
        def one(i):
            body((along[axis] + near_first(i)) % SIDE)

        loop(0, SIDE - 1, one)

    for axis in axes:
        own = along[axis]
        to_line(axis, lambda f: send(
            meta.at[axis, own], meta.at[axis, own], meta_send.at[axis, f], meta_recv.at[axis, own],
            on_line(axis, f),
        ))
    blocks[second, first] = heads[...]
    for kv in range(2):
        def pass_on(i):
            f = (first + near_first(i)) % SIDE
            wait(blocks.at[second, f, :, side(kv)], first_recv.at[kv, f])
            start_second(kv, f, blocks.at[second, f, :, side(kv)])

        loop(0, SIDE - 1, pass_on)
    own_weight.wait()
    wait(weight, head_weight_sems.at[2])
    mine = pl.ds(pl.multiple_of((z * SIDE + x) * 256, 256), 256)

    def project(s):
        rows = blocks[s].reshape(SIDE * tokens, width)
        products[s] = exact(rows, columns_held[...]).astype(jnp.bfloat16).reshape(SIDE, tokens, 256)

    def back(f, s):
        send(
            products.at[s, f], projected.at[:, mine], back_send.at[s, f],
            back_recv.at[second, first], at(f, s),
        )

    project(second)
    projected[:, mine] = products[second, first]
    loop(0, SIDE - 1, lambda i: back((first + near_first(i)) % SIDE, second))

    for axis in axes:
        q = iota((1, 512), 1)
        target = ordered(axis, q >> 4, shifted(q, 1, SIDE), q & 1) + shifted(q, 3, 2) * 256
        gather[axis] = ones_where(iota((512, 512), 0) == target)
        q = iota((256, 1), 0)
        target = ordered(axis, q >> 3, shifted(q, 1, SIDE), q & 1)
        spread[axis] = ones_where(iota((256, 256), 1) == target)

    for axis in axes:
        to_line(axis, lambda f: wait(meta.at[axis, 0], meta_recv.at[axis, f]))
        known = meta[axis].reshape(SIDE * 16, 256)
        present = ones_where(known.astype(jnp.float32) > 0.0)

        def expert(p):
            ex, ey, ez = spot(axis, shifted(p, 3, SIDE), shifted(p, 1, SIDE), along[axis])
            return (ey * SIDE + ez) * (2 * SIDE) + ex * 2 + (p & 1)

        q = iota((256, 1), 0)
        wanted = ones_where(iota((256, 256), 1) == (q & 1) * 128 + expert(q >> 3))
        chosen = lax.dot_general(wanted, present, nt, preferred_element_type=jnp.float32)
        same = shifted(q, 1, SIDE) == iota((1, SIDE * 16), 1) >> 4
        choose[axis] = jnp.where(same, chosen, 0.0).astype(jnp.bfloat16)
        q = iota((512, 1), 0)
        wanted = ones_where(iota((512, 256), 1) == (q & 1) * 128 + expert(q >> 4))
        scaled = lax.dot_general(known, wanted, nt, preferred_element_type=jnp.float32)
        q = iota((1, 512), 1)
        scaled = jnp.where(iota((SIDE * 16, 1), 0) >> 4 == shifted(q, 1, SIDE), scaled, 0.0)
        upper = shifted(q, 3, 2) == 0
        weigh[axis] = jnp.concatenate(
            [jnp.where(upper, scaled, 0.0), jnp.where(upper, 0.0, scaled)], axis=0
        ).astype(jnp.bfloat16)

    def other_group(i):
        s = (second + near_first(i)) % SIDE

        def arrived(f):
            for kv in range(2):
                wait(blocks.at[s, f, :, side(kv)], second_recv.at[kv, s, f])

        loop(0, SIDE, arrived)
        project(s)
        loop(0, SIDE, lambda f: back(f, s))

    loop(0, SIDE - 1, other_group)

    def others_in_plane(body):
        def one(i):
            other = (second * SIDE + first + i) % (SIDE * SIDE)
            body(other % SIDE, other // SIDE)

        loop(1, SIDE * SIDE, one)

    others_in_plane(lambda f, s: wait(products.at[s, f], back_recv.at[s, f]))
    loads[3].wait()
    added = residual[...].astype(jnp.float32) + projected[...].astype(jnp.float32)
    rounded = added.astype(jnp.bfloat16)
    attended[...] = rounded
    stream = rounded.astype(jnp.float32)
    level = lax.rsqrt(jnp.mean(stream * stream, axis=-1, keepdims=True) + EPSILON)
    normed[...] = (stream * level * moe_gain[...]).astype(jnp.bfloat16)
    for axis in axes:
        own = along[axis]
        to_line(axis, lambda f: send(
            normed.at[:, columns(axis)], shared.at[own, :, columns(axis)],
            share_send.at[axis, f], share_recv.at[axis, own], on_line(axis, f),
        ))
        shared[along[axis], :, columns(axis)] = normed[:, columns(axis)]

    def dispatch(part, axis):
        loop(1, PLANE, lambda i: send(
            picked.at[partner(axis, i), :, lanes(part, axis)], received.at[index[axis], :, lanes(part, axis)],
            out_send.at[part, axis], out_recv.at[part, axis], in_plane(axis, partner(axis, i)),
        ))

    for axis in axes:
        to_line(axis, lambda f: wait(shared.at[0, :, columns(axis)], share_recv.at[axis, f]))
        rows = shared[:, :, columns(axis)].reshape(SIDE * 16, GROUPS[axis][1])
        result = jnp.dot(choose[axis], rows, preferred_element_type=jnp.float32)
        base, width = GROUPS[axis]
        picked[:, :, pl.ds(base // 2, width // 2)] = halves(result)
        dispatch(0, axis)
    for part in range(1, len(PARTS)):
        each_partner(lambda axis, p: send(
            picked.at[p, :, lanes(part, axis)], received.at[index[axis], :, lanes(part, axis)],
            out_send.at[part, axis], out_recv.at[part, axis], in_plane(axis, p),
        ))
    for axis in axes:
        base, width = GROUPS[axis]
        whole = pl.ds(base // 2, width // 2)
        received[index[axis], :, whole] = picked[index[axis], :, whole]

    hidden_size = down.shape[1]
    many = pl.ds(0, PLANE - 1)
    for part in range(len(PARTS)):
        for axis in axes:
            wait(received.at[many, :, lanes(part, axis)], out_recv.at[part, axis])
            if part == 0:
                fetches[axis].wait()
            size = PARTS[part][axis][1]
            messages = received[:, :, lanes(part, axis)].reshape(PLANE * 16, size)
            rows = jnp.dot(gather[axis], messages, preferred_element_type=jnp.float32)
            rows = rows.astype(jnp.bfloat16)
            upper, lower = both_columns(part, axis)

            def step(n):
                piece = pl.ds(pl.multiple_of(n * 512, 512), 512)
                product = jnp.dot(
                    rows[:256], gate_up_held[upper, piece], preferred_element_type=jnp.float32
                ) + jnp.dot(
                    rows[256:], gate_up_held[lower, piece], preferred_element_type=jnp.float32
                )
                if part == 0 and axis == 0:
                    total[:, piece] = product
                else:
                    total[:, piece] += product

            loop(0, 2 * hidden_size // 512, step)

    gate = total[:, :hidden_size]
    hidden = (gate / (1.0 + jnp.exp(-gate)) * total[:, hidden_size:]).astype(jnp.bfloat16)
    for axis in axes:
        fetches[3 + axis].wait()
    hiddens = [
        jnp.dot(spread[axis], hidden, preferred_element_type=jnp.float32).astype(jnp.bfloat16)
        for axis in axes
    ]
    for part in range(len(PARTS)):
        for axis in axes:
            upper, lower = both_columns(part, axis)
            result = [
                jnp.dot(hiddens[axis], down_held[:, cols], preferred_element_type=jnp.float32)
                for cols in (upper, lower)
            ]
            answers[:, :, lanes(part, axis)] = halves(jnp.concatenate(result, axis=1))
        each_partner(lambda axis, p: send(
            answers.at[p, :, lanes(part, axis)], returned.at[index[axis], :, lanes(part, axis)],
            ret_send.at[part, axis], ret_recv.at[part, axis], in_plane(axis, p),
        ))
        for axis in axes:
            returned[index[axis], :, lanes(part, axis)] = answers[index[axis], :, lanes(part, axis)]

    for part in range(len(PARTS)):
        for axis in axes:
            wait(returned.at[many, :, lanes(part, axis)], ret_recv.at[part, axis])
            size = PARTS[part][axis][1]
            messages = returned[:, :, lanes(part, axis)].reshape(PLANE * 16, size)
            result = jnp.dot(weigh[axis], messages, preferred_element_type=jnp.float32)
            result = result.astype(jnp.bfloat16).reshape(2, SIDE, 16, size)
            upper, lower = both_columns(part, axis)
            partial[:, :, upper] = result[0]
            partial[:, :, lower] = result[1]
            if part == len(PARTS) - 1:
                own = along[axis]
                to_line(axis, lambda f: send(
                    partial.at[f, :, columns(axis)], landed.at[own, :, columns(axis)],
                    sum_send.at[axis, f], sum_recv.at[axis, own], on_line(axis, f),
                ))
    for axis in axes:
        to_line(axis, lambda f: wait(landed.at[0, :, columns(axis)], sum_recv.at[axis, f]))
        own = along[axis]
        block = partial[own, :, columns(axis)].astype(jnp.float32)
        for d in range(1, SIDE):
            block = block + landed[(own + d) % SIDE, :, columns(axis)].astype(jnp.float32)
        block = block + attended[:, columns(axis)].astype(jnp.float32)
        mixed[:, columns(axis)] = block.astype(jnp.bfloat16)

    wait(weight, head_weight_sems.at[1])
    for kv in range(2):
        def finish_first(i):
            f = (first + 1 + i) % SIDE
            s = (second + 1 + i) % SIDE
            wait(heads.at[:, side(kv)], first_send.at[kv, f])
            loop(0, SIDE, lambda g: wait(heads.at[:, side(kv)], second_send.at[kv, s, g]))

        loop(0, SIDE - 1, finish_first)
    others_in_plane(lambda f, s: wait(products.at[s, f], back_send.at[s, f]))
    for axis in axes:
        to_line(axis, lambda f: wait(meta.at[axis, 0], meta_send.at[axis, f]))
        to_line(axis, lambda f: wait(landed.at[0, :, columns(axis)], share_send.at[axis, f]))
        to_line(axis, lambda f: wait(landed.at[0, :, columns(axis)], sum_send.at[axis, f]))
        for part in range(len(PARTS)):
            wait(picked.at[many, :, lanes(part, axis)], out_send.at[part, axis])
            wait(answers.at[many, :, lanes(part, axis)], ret_send.at[part, axis])


def local(
    residual,
    query,
    new_key_value,
    cached_key_rows,
    cached_value_rows,
    lengths,
    q_gain,
    k_gain,
    out_weight,
    moe_gain,
    expert_ids,
    gate_probs,
    expert_gate_up,
    expert_down,
):
    rows, width = residual.shape
    hidden = expert_down.shape[1]
    slots = cached_key_rows.shape[1]
    vmem = pl.BlockSpec(memory_space=pltpu.VMEM)
    hbm = pl.BlockSpec(memory_space=pltpu.HBM)
    sems = pltpu.SemaphoreType.DMA
    bf16 = jnp.bfloat16
    own = pltpu.VMEM((rows, width), bf16)
    caches = pltpu.VMEM(cached_key_rows.shape, bf16)
    messages = pltpu.VMEM((PLANE, 16, width // 2), bf16)
    lines = pltpu.VMEM((SIDE, rows, width), bf16)
    parts = len(PARTS)
    both = pl.pallas_call(
        kernel,
        out_shape=jax.ShapeDtypeStruct((2, rows, width), bf16),
        in_specs=[hbm] * 14,
        out_specs=vmem,
        scratch_shapes=[
            own,
            caches,
            caches,
            own,
            pltpu.VMEM(new_key_value.shape, bf16),
            pltpu.VMEM((1, rows), jnp.int32),
            pltpu.VMEM((1, 128), jnp.float32),
            pltpu.VMEM((1, 128), jnp.float32),
            pltpu.VMEM((1, width), jnp.float32),
            pltpu.VMEM((expert_ids.shape[1], rows), jnp.int32),
            pltpu.VMEM((expert_ids.shape[1], rows), jnp.float32),
            pltpu.VMEM((2, 256, slots), jnp.float32),
            pltpu.VMEM((256, 128), jnp.float32),
            own,
            pltpu.VMEM((width, 256), bf16),
            pltpu.VMEM((SIDE, SIDE, rows, width), bf16),
            pltpu.VMEM((SIDE, SIDE, rows, 256), bf16),
            own,
            own,
            pltpu.VMEM((width, 2 * hidden), bf16),
            pltpu.VMEM((hidden, width), bf16),
            pltpu.VMEM((3, SIDE, rows, 256), bf16),
            lines,
            messages,
            messages,
            pltpu.VMEM((256, 2 * hidden), jnp.float32),
            messages,
            messages,
            lines,
            lines,
            pltpu.VMEM((3, 256, SIDE * rows), bf16),
            pltpu.VMEM((3, 2 * SIDE * rows, 512), bf16),
            pltpu.VMEM((3, 512, 512), bf16),
            pltpu.VMEM((3, 256, 256), bf16),
            sems((11,)),
            sems((3,)),
            sems((2, SIDE)),
            sems((2, SIDE)),
            sems((2, SIDE, SIDE)),
            sems((2, SIDE, SIDE)),
            sems((SIDE, SIDE)),
            sems((SIDE, SIDE)),
            sems((6,)),
            sems((3, SIDE)),
            sems((3, SIDE)),
            sems((3, SIDE)),
            sems((3, SIDE)),
            sems((parts, 3)),
            sems((parts, 3)),
            sems((parts, 3)),
            sems((parts, 3)),
            sems((3, SIDE)),
            sems((3, SIDE)),
        ],
        compiler_params=pltpu.CompilerParams(
            collective_id=1, has_side_effects=True, vmem_limit_bytes=60 << 20
        ),
        name="layer",
    )(
        residual, query, new_key_value, cached_key_rows, cached_value_rows,
        lengths.reshape(1, rows), q_gain.reshape(1, 128), k_gain.reshape(1, 128), out_weight,
        moe_gain.reshape(1, width), expert_ids.T, gate_probs.T, expert_gate_up, expert_down,
    )
    return (both[0], both[1])


def solution(mesh):
    return jax.shard_map(
        local,
        mesh=mesh,
        in_specs=(
            P(("dp", "ep"), None),
            P(("dp", "ep"), None),
            P(("dp", "ep"), None, None),
            P(("dp", "ep"), None, None),
            P(("dp", "ep"), None, None),
            P(("dp", "ep")),
            P(),
            P(),
            P(None, "ep"),
            P(),
            P(("dp", "ep"), None),
            P(("dp", "ep"), None),
            P(("dp", "ep"), None, None),
            P(("dp", "ep"), None, None),
        ),
        out_specs=(P(("dp", "ep"), None), P(("dp", "ep"), None)),
        check_vma=False,
    )
```

```python
import math

import jax
import jax.numpy as jnp
from jax import lax
from jax.experimental import pallas as pl
from jax.experimental.pallas import tpu as pltpu
from jax.sharding import PartitionSpec as P

EPSILON = 1e-06
THETA = 1000000.0


MESH = pl.DeviceIdType.MESH
SIDE = 4
PLANE = 2 * SIDE * SIDE
GROUPS = ((0, 1280), (1280, 1536), (2816, 1280))
PARTS = (
    ((0, 256), (0, 256), (0, 256)),
    ((256, 256), (256, 256), (256, 256)),
    ((512, 128), (512, 256), (512, 128)),
)


def place():
    y = lax.axis_index("dp")
    e = lax.axis_index("ep")
    return (e // 2) % SIDE, y, e // (2 * SIDE), e % 2


def device(x, y, z, core):
    return (y, (z * SIDE + x) * 2 + core)


def signal(target):
    pl.semaphore_signal(
        pltpu.get_barrier_semaphore(), inc=1, device_id=target, device_id_type=MESH
    )


def send(source, target, send_sem, recv_sem, where):
    pltpu.make_async_remote_copy(
        src_ref=source,
        dst_ref=target,
        send_sem=send_sem,
        recv_sem=recv_sem,
        device_id=where,
        device_id_type=MESH,
    ).start()


def wait(ref, sem):
    pltpu.make_async_copy(ref, ref, sem).wait()


def loop(first, last, body):
    def step(i, carry):
        body(i)
        return carry

    lax.fori_loop(first, last, step, 0)


def near_first(i):
    return 1 + 2 * i - 3 * (i // 2)


def route(ids, probs):
    top, count = ids.shape
    experts = 128
    weights = probs / jnp.sum(probs, axis=0, keepdims=True)
    label = iota((experts, count), 0)
    named = jnp.zeros((experts, count), jnp.float32)
    value = jnp.zeros((experts, count), jnp.float32)
    for k in range(top):
        match = ids[k : k + 1] == label
        named = named + jnp.where(match, 1.0, 0.0)
        value = value + jnp.where(match, weights[k : k + 1], 0.0)
    before = jnp.where(iota((count, count), 0) < iota((count, count), 1), 1.0, 0.0)
    earlier = jnp.dot(named, before, preferred_element_type=jnp.float32)
    again = earlier > 0.5
    both = jnp.concatenate(
        [jnp.where(again, 0.0, value), jnp.where(again, value, 0.0)], axis=0
    )
    return both.T.astype(jnp.bfloat16)


def turned(rows, cosines, sines, gain):
    mean_square = jnp.mean(rows * rows, axis=-1, keepdims=True)
    scaled = rows * lax.rsqrt(mean_square + EPSILON) * gain
    return (scaled * cosines + pltpu.roll(scaled, 64, 1) * sines).astype(jnp.bfloat16)


def halves(rows):
    width = rows.shape[1] // 2
    parts = rows.reshape(PLANE, 8, 2 * width)
    return jnp.concatenate([parts[:, :, :width], parts[:, :, width:]], axis=1).astype(jnp.bfloat16)


def iota(shape, dim):
    return lax.broadcasted_iota(jnp.int32, shape, dim)


def shifted(value, by, size):
    return (value >> by) & (size - 1)


def spot(axis, a, b, f):
    return ((f, a, b), (b, f, a), (b, a, f))[axis]


def ordered(axis, p, f, slot):
    x, y, z = spot(axis, shifted(p, 3, SIDE), shifted(p, 1, SIDE), f)
    return ((y * SIDE + z) * SIDE + x) * 4 + (p & 1) * 2 + slot


def ones_where(condition):
    return jnp.where(condition, 1.0, 0.0).astype(jnp.bfloat16)


def kernel(
    residual_in, query_in, new_in, keys_in, values_in, lengths_in, q_gain_in, k_gain_in, weight, moe_gain_in,
    ids_in, probs_in, gate_up, down, out,
    query, keys, values, residual, new, lengths, q_gain, k_gain, moe_gain, ids, probs, scores, products_pv, heads, columns_held, blocks, products, projected,
    normed, gate_up_held, down_held, meta, shared, picked, received, ordered_rows, total, answers, returned,
    partial, landed, choose, weigh, gather, spread,
    cache_sems, head_weight_sems, first_send, first_recv, second_send, second_recv, relay_send, back_send, back_recv,
    weight_sems, meta_send, meta_recv, share_send, share_recv, out_send, out_recv,
    ret_send, ret_recv, sum_send, sum_recv,
):
    attended, mixed = out.at[0], out.at[1]
    x, y, z, core = place()
    along = (x, y, z)
    across = ((y, z), (z, x), (y, x))
    axes = range(3)
    index = [(a * SIDE + b) * 2 + core for a, b in across]

    def on_line(axis, f):
        return device(*[f if i == axis else along[i] for i in axes], core)

    def in_plane(axis, p):
        return device(*spot(axis, p // (2 * SIDE), (p // 2) % SIDE, along[axis]), p % 2)

    def partner(axis, i):
        step = (13 * i) % PLANE
        a, b = across[axis]
        return (((a + step // (2 * SIDE)) % SIDE) * SIDE + (b + step // 2) % SIDE) * 2 + (core + step) % 2

    def each_partner(body):
        def one(i):
            for axis in axes:
                body(axis, partner(axis, i))

        loop(1, PLANE, one)

    def columns(axis):
        return pl.ds(*GROUPS[axis])

    def lanes(part, axis):
        start, size = PARTS[part][axis]
        return pl.ds(GROUPS[axis][0] // 2 + start, size)

    def both_columns(part, axis):
        start, size = PARTS[part][axis]
        base, width = GROUPS[axis]
        return pl.ds(base + start, size), pl.ds(base + width // 2 + start, size)

    loads = [
        pltpu.make_async_copy(source, target, cache_sems.at[i])
        for i, (source, target) in enumerate(
            (
                (query_in, query), (keys_in, keys), (values_in, values), (residual_in, residual),
                (new_in, new), (lengths_in, lengths), (q_gain_in, q_gain), (k_gain_in, k_gain),
                (moe_gain_in, moe_gain), (ids_in, ids), (probs_in, probs),
            )
        )
    ]
    for i in (0, 4, 5, 6, 7, 1, 2, 9, 10, 8, 3):
        loads[i].start()
    half = pl.ds(pl.multiple_of(core * 128, 128), 128)
    own_weight = pltpu.make_async_copy(weight, columns_held.at[:, half], head_weight_sems.at[0])
    own_weight.start()
    def greet(i):
        other = (z * SIDE + x + i) % (SIDE * SIDE)
        signal(device(other % SIDE, y, other // SIDE, core))

    def greet_row(i):
        row = (y + i) % SIDE
        signal(device(x, row, z, core))
        signal(device(x, row, z, 1 - core))

    signal(device(x, y, z, 1 - core))
    loop(1, SIDE * SIDE, greet)
    loop(1, SIDE, greet_row)
    order, place_of = [], {}
    for part in range(len(PARTS)):
        for axis in axes:
            for h, cols in enumerate(both_columns(part, axis)):
                place_of[part, axis, h] = pl.ds(sum(c.size for c in order), cols.size)
                order.append(cols)
    gate_up_fetches = [
        pltpu.make_async_copy(gate_up.at[0, cols], gate_up_held.at[to], weight_sems.at[3 + i])
        for i, (cols, to) in enumerate(zip(order, place_of.values()))
    ]
    fetches = gate_up_fetches + [
        pltpu.make_async_copy(down.at[0, :, cols], down_held.at[:, cols], weight_sems.at[i])
        for i, cols in enumerate([pl.ds(*group) for group in GROUPS])
    ]
    for fetch in fetches:
        fetch.start()
    for load in loads[4:8]:
        load.wait()
    tokens, slots, group = 16, keys.shape[1], 16
    pairs = tokens * group
    nt = (((1,), (1,)), ((), ()))

    def exact(left, right, dims=(((1,), (0,)), ((), ()))):
        return lax.dot_general(left, right, dims, preferred_element_type=jnp.float32)

    count = jnp.broadcast_to(lengths[...].astype(jnp.float32), (128, tokens)).astype(jnp.bfloat16)
    same_token = ones_where(iota((pairs, tokens), 0) >> 4 == iota((pairs, tokens), 1))
    eye = ones_where(iota((tokens, tokens), 0) == iota((tokens, tokens), 1))
    position = exact(eye, count, nt)
    lane = iota((tokens, 128), 1)
    freqs = jnp.exp((lane & 63).astype(jnp.float32) * (-2.0 * math.log(THETA) / 128))
    angles = position * freqs
    cosines = jnp.cos(angles)
    sines = jnp.where(lane < 64, -1.0, 1.0) * jnp.sin(angles)
    row, col = iota((pairs, pairs), 0), iota((pairs, pairs), 1)
    swap = ones_where(((row >> 4) == (col & 15)) & ((row & 15) == (col >> 4)))
    live = iota((pairs, slots), 1) < jnp.concatenate(
        [exact(same_token, count, nt)] * (slots // 128), axis=1
    ).astype(jnp.int32)
    scale = 1.0 / math.sqrt(128)
    many_cosines = jnp.concatenate([cosines] * group, axis=0)
    many_sines = jnp.concatenate([sines] * group, axis=0)
    loads[0].wait()

    def score(kv):
        stack = jnp.concatenate(
            [query[:, (kv * group + h) * 128 : (kv * group + h + 1) * 128] for h in range(group)], axis=0
        ).astype(jnp.float32)
        rotated = exact(swap, turned(stack, many_cosines, many_sines, q_gain[...]))
        new_key = turned(
            new[:, 0, kv * 128 : kv * 128 + 128].astype(jnp.float32), cosines, sines, k_gain[...]
        )
        own = jnp.sum(rotated * exact(same_token, new_key), axis=-1, keepdims=True) * scale
        queries = rotated.astype(jnp.bfloat16)
        if kv == 0:
            loads[1].wait()
        for t in range(tokens):
            scores[kv, t * group : (t + 1) * group] = exact(
                queries[t * group : (t + 1) * group], keys[t, :, kv * 128 : kv * 128 + 128], nt
            )
        return own

    def attend(kv):
        lanes_of = slice(kv * 128, kv * 128 + 128)
        own = score(kv)
        masked = jnp.where(live, scores[kv] * scale, -jnp.inf)
        highest = jnp.maximum(jnp.max(masked, axis=-1, keepdims=True), own)
        expos = jnp.exp(masked - highest)
        own_expo = jnp.exp(own - highest)
        sums = jnp.sum(expos, axis=-1, keepdims=True) + own_expo
        probs_of = (expos / sums).astype(jnp.bfloat16)
        own_prob = (own_expo / sums).astype(jnp.bfloat16).astype(jnp.float32)
        if kv == 0:
            loads[2].wait()
        for t in range(tokens):
            products_pv[t * group : (t + 1) * group] = exact(
                probs_of[t * group : (t + 1) * group], values[t, :, lanes_of]
            )
        new_value = exact(same_token, new[:, 1, kv * 128 : kv * 128 + 128])
        result = (products_pv[...] + own_prob * new_value).astype(jnp.bfloat16)
        result = exact(swap, result).astype(jnp.bfloat16)
        for h in range(group):
            heads[:, (kv * group + h) * 128 : (kv * group + h + 1) * 128] = result[
                h * tokens : (h + 1) * tokens
            ]

    first = x * (1 - core) + z * core
    second = z * (1 - core) + x * core

    def at(f, s):
        return device(f * (1 - core) + s * core, y, s * (1 - core) + f * core, core)

    width = heads.shape[1]
    wide = width // 2

    def side(kv):
        return pl.ds(kv * wide, wide)

    def start_first(kv):
        def one(i):
            f = (first + near_first(i)) % SIDE
            send(
                heads.at[:, side(kv)], blocks.at[second, first, :, side(kv)],
                first_send.at[kv, f], first_recv.at[kv, first], at(f, second),
            )

        loop(0, SIDE - 1, one)

    def start_second(kv, f, source):
        def one(i):
            s = (second + near_first(i)) % SIDE
            send(
                source, blocks.at[second, f, :, side(kv)], second_send.at[kv, s, f],
                second_recv.at[kv, second, f], at(first, s),
            )

        loop(0, 2, one)

    sibling = device(x, y, z, 1 - core)
    attend(0)
    pl.semaphore_wait(pltpu.get_barrier_semaphore(), SIDE * SIDE + 2 * (SIDE - 1))
    start_first(0)
    start_second(0, first, heads.at[:, side(0)])
    attend(1)
    start_first(1)
    start_second(1, first, heads.at[:, side(1)])
    send(weight, columns_held.at[:, half], head_weight_sems.at[1], head_weight_sems.at[2], sibling)

    loads[9].wait()
    loads[10].wait()
    own_meta = route(ids[...], probs[...])
    for axis in axes:
        meta[axis, along[axis]] = own_meta

    def to_line(axis, body):
        def one(i):
            body((along[axis] + near_first(i)) % SIDE)

        loop(0, SIDE - 1, one)

    for axis in axes:
        own = along[axis]
        to_line(axis, lambda f: send(
            meta.at[axis, own], meta.at[axis, own], meta_send.at[axis, f], meta_recv.at[axis, own],
            on_line(axis, f),
        ))
    blocks[second, first] = heads[...]
    for kv in range(2):
        def pass_on(i):
            f = (first + near_first(i)) % SIDE
            wait(blocks.at[second, f, :, side(kv)], first_recv.at[kv, f])
            start_second(kv, f, blocks.at[second, f, :, side(kv)])

        loop(0, SIDE - 1, pass_on)
    before, after = (second + SIDE - 1) % SIDE, (second + 1) % SIDE

    def relay(kv, f):
        origin, to = ((before, after), (after, before))[kv]
        piece = blocks.at[origin, f, :, side(kv)]
        wait(piece, second_recv.at[kv, origin, f])
        send(piece, piece, relay_send.at[kv, f], second_recv.at[kv, origin, f], at(first, to))

    for kv in range(2):
        relay(kv, first)
    for kv in range(2):
        loop(0, SIDE - 1, lambda i: relay(kv, (first + near_first(i)) % SIDE))
    own_weight.wait()
    wait(weight, head_weight_sems.at[2])
    mine = pl.ds(pl.multiple_of((z * SIDE + x) * 256, 256), 256)

    def project(s):
        rows = blocks[s].reshape(SIDE * tokens, width)
        products[s] = exact(rows, columns_held[...]).astype(jnp.bfloat16).reshape(SIDE, tokens, 256)

    def back(f, s):
        send(
            products.at[s, f], projected.at[:, mine], back_send.at[s, f],
            back_recv.at[second, first], at(f, s),
        )

    project(second)
    projected[:, mine] = products[second, first]
    loop(0, SIDE - 1, lambda i: back((first + near_first(i)) % SIDE, second))

    for axis in axes:
        q = iota((1, 256), 1)
        target = ordered(axis, q >> 3, shifted(q, 1, SIDE), q & 1)
        gather[axis] = ones_where(iota((256, 256), 0) == target)
        q = iota((256, 1), 0)
        target = ordered(axis, q >> 3, shifted(q, 1, SIDE), q & 1)
        spread[axis] = ones_where(iota((256, 256), 1) == target)

    for axis in axes:
        to_line(axis, lambda f: wait(meta.at[axis, 0], meta_recv.at[axis, f]))
        known = meta[axis].reshape(SIDE * 16, 256)
        present = ones_where(known.astype(jnp.float32) > 0.0)

        def expert(p):
            ex, ey, ez = spot(axis, shifted(p, 3, SIDE), shifted(p, 1, SIDE), along[axis])
            return (ey * SIDE + ez) * (2 * SIDE) + ex * 2 + (p & 1)

        q = iota((256, 1), 0)
        wanted = ones_where(iota((256, 256), 1) == (q & 1) * 128 + expert(q >> 3))
        chosen = lax.dot_general(wanted, present, nt, preferred_element_type=jnp.float32)
        same = shifted(q, 1, SIDE) == iota((1, SIDE * 16), 1) >> 4
        choose[axis] = jnp.where(same, chosen, 0.0).astype(jnp.bfloat16)
        q = iota((512, 1), 0)
        wanted = ones_where(iota((512, 256), 1) == (q & 1) * 128 + expert(q >> 4))
        scaled = lax.dot_general(known, wanted, nt, preferred_element_type=jnp.float32)
        q = iota((1, 512), 1)
        scaled = jnp.where(iota((SIDE * 16, 1), 0) >> 4 == shifted(q, 1, SIDE), scaled, 0.0)
        upper = shifted(q, 3, 2) == 0
        weigh[axis] = jnp.concatenate(
            [jnp.where(upper, scaled, 0.0), jnp.where(upper, 0.0, scaled)], axis=0
        ).astype(jnp.bfloat16)

    def group_of(s, halves_left):
        for kv in halves_left:
            loop(0, SIDE, lambda f: wait(blocks.at[s, f, :, side(kv)], second_recv.at[kv, s, f]))
        project(s)
        loop(0, SIDE, lambda f: back(f, s))

    group_of(before, (1,))
    group_of(after, (0,))
    group_of((second + 2) % SIDE, (0, 1))

    def others_in_plane(body):
        def one(i):
            other = (second * SIDE + first + i) % (SIDE * SIDE)
            body(other % SIDE, other // SIDE)

        loop(1, SIDE * SIDE, one)

    others_in_plane(lambda f, s: wait(products.at[s, f], back_recv.at[s, f]))
    loads[3].wait()
    loads[8].wait()
    added = residual[...].astype(jnp.float32) + projected[...].astype(jnp.float32)
    rounded = added.astype(jnp.bfloat16)
    attended[...] = rounded
    stream = rounded.astype(jnp.float32)
    level = lax.rsqrt(jnp.mean(stream * stream, axis=-1, keepdims=True) + EPSILON)
    normed[...] = (stream * level * moe_gain[...]).astype(jnp.bfloat16)
    for axis in axes:
        own = along[axis]
        to_line(axis, lambda f: send(
            normed.at[:, columns(axis)], shared.at[own, :, columns(axis)],
            share_send.at[axis, f], share_recv.at[axis, own], on_line(axis, f),
        ))
        shared[along[axis], :, columns(axis)] = normed[:, columns(axis)]

    def dispatch(part, axis):
        loop(1, PLANE, lambda i: send(
            picked.at[partner(axis, i), :, lanes(part, axis)], received.at[index[axis], :, lanes(part, axis)],
            out_send.at[part, axis], out_recv.at[part, axis], in_plane(axis, partner(axis, i)),
        ))

    for axis in axes:
        to_line(axis, lambda f: wait(shared.at[0, :, columns(axis)], share_recv.at[axis, f]))
        rows = shared[:, :, columns(axis)].reshape(SIDE * 16, GROUPS[axis][1])
        result = jnp.dot(choose[axis], rows, preferred_element_type=jnp.float32)
        base, width = GROUPS[axis]
        picked[:, :, pl.ds(base // 2, width // 2)] = halves(result)
        dispatch(0, axis)
    for part in range(1, len(PARTS)):
        each_partner(lambda axis, p: send(
            picked.at[p, :, lanes(part, axis)], received.at[index[axis], :, lanes(part, axis)],
            out_send.at[part, axis], out_recv.at[part, axis], in_plane(axis, p),
        ))
    for axis in axes:
        base, width = GROUPS[axis]
        whole = pl.ds(base // 2, width // 2)
        received[index[axis], :, whole] = picked[index[axis], :, whole]

    hidden_size = down.shape[1]
    many = pl.ds(0, PLANE - 1)
    for part in range(len(PARTS)):
        for axis in axes:
            wait(received.at[many, :, lanes(part, axis)], out_recv.at[part, axis])
            size = PARTS[part][axis][1]
            messages = received[:, :, lanes(part, axis)].astype(jnp.float32)
            for h in range(2):
                rows = messages[:, h * 8 : h * 8 + 8].reshape(PLANE * 8, size).astype(jnp.bfloat16)
                rows = jnp.dot(gather[axis], rows, preferred_element_type=jnp.float32)
                ordered_rows[:, place_of[part, axis, h]] = rows.astype(jnp.bfloat16)
        for fetch in gate_up_fetches[6 * part : 6 * part + 6]:
            fetch.wait()
        start = place_of[part, 0, 0].start
        depth = pl.ds(start, 2 * sum(p[1] for p in PARTS[part]))

        def step(n):
            piece = pl.ds(pl.multiple_of(n * 768, 768), 768)
            product = jnp.dot(
                ordered_rows[:, depth], gate_up_held[depth, piece], preferred_element_type=jnp.float32
            )
            if part == 0:
                total[:, piece] = product
            else:
                total[:, piece] += product

        loop(0, 2 * hidden_size // 768, step)

    gate = total[:, :hidden_size]
    hidden = (gate / (1.0 + jnp.exp(-gate)) * total[:, hidden_size:]).astype(jnp.bfloat16)
    for axis in axes:
        fetches[len(order) + axis].wait()
    hiddens = [
        jnp.dot(spread[axis], hidden, preferred_element_type=jnp.float32).astype(jnp.bfloat16)
        for axis in axes
    ]
    for part in range(len(PARTS)):
        for axis in axes:
            upper, lower = both_columns(part, axis)
            result = [
                jnp.dot(hiddens[axis], down_held[:, cols], preferred_element_type=jnp.float32)
                for cols in (upper, lower)
            ]
            answers[:, :, lanes(part, axis)] = halves(jnp.concatenate(result, axis=1))
        each_partner(lambda axis, p: send(
            answers.at[p, :, lanes(part, axis)], returned.at[index[axis], :, lanes(part, axis)],
            ret_send.at[part, axis], ret_recv.at[part, axis], in_plane(axis, p),
        ))
        for axis in axes:
            returned[index[axis], :, lanes(part, axis)] = answers[index[axis], :, lanes(part, axis)]

    for part in range(len(PARTS)):
        for axis in axes:
            wait(returned.at[many, :, lanes(part, axis)], ret_recv.at[part, axis])
            size = PARTS[part][axis][1]
            messages = returned[:, :, lanes(part, axis)].reshape(PLANE * 16, size)
            result = jnp.dot(weigh[axis], messages, preferred_element_type=jnp.float32)
            result = result.astype(jnp.bfloat16).reshape(2, SIDE, 16, size)
            upper, lower = both_columns(part, axis)
            partial[:, :, upper] = result[0]
            partial[:, :, lower] = result[1]
            if part == len(PARTS) - 1:
                own = along[axis]
                to_line(axis, lambda f: send(
                    partial.at[f, :, columns(axis)], landed.at[own, :, columns(axis)],
                    sum_send.at[axis, f], sum_recv.at[axis, own], on_line(axis, f),
                ))
    for axis in axes:
        to_line(axis, lambda f: wait(landed.at[0, :, columns(axis)], sum_recv.at[axis, f]))
        own = along[axis]
        block = partial[own, :, columns(axis)].astype(jnp.float32)
        for d in range(1, SIDE):
            block = block + landed[(own + d) % SIDE, :, columns(axis)].astype(jnp.float32)
        block = block + attended[:, columns(axis)].astype(jnp.float32)
        mixed[:, columns(axis)] = block.astype(jnp.bfloat16)

    wait(weight, head_weight_sems.at[1])
    for kv in range(2):
        loop(1, SIDE, lambda i: wait(heads.at[:, side(kv)], first_send.at[kv, (first + i) % SIDE]))
        for s in (before, after):
            loop(0, SIDE, lambda g: wait(heads.at[:, side(kv)], second_send.at[kv, s, g]))
        loop(0, SIDE, lambda g: wait(heads.at[:, side(kv)], relay_send.at[kv, g]))
    others_in_plane(lambda f, s: wait(products.at[s, f], back_send.at[s, f]))
    for axis in axes:
        to_line(axis, lambda f: wait(meta.at[axis, 0], meta_send.at[axis, f]))
        to_line(axis, lambda f: wait(landed.at[0, :, columns(axis)], share_send.at[axis, f]))
        to_line(axis, lambda f: wait(landed.at[0, :, columns(axis)], sum_send.at[axis, f]))
        for part in range(len(PARTS)):
            wait(picked.at[many, :, lanes(part, axis)], out_send.at[part, axis])
            wait(answers.at[many, :, lanes(part, axis)], ret_send.at[part, axis])


def local(
    residual,
    query,
    new_key_value,
    cached_key_rows,
    cached_value_rows,
    lengths,
    q_gain,
    k_gain,
    out_weight,
    moe_gain,
    expert_ids,
    gate_probs,
    expert_gate_up,
    expert_down,
):
    rows, width = residual.shape
    hidden = expert_down.shape[1]
    slots = cached_key_rows.shape[1]
    vmem = pl.BlockSpec(memory_space=pltpu.VMEM)
    hbm = pl.BlockSpec(memory_space=pltpu.HBM)
    sems = pltpu.SemaphoreType.DMA
    bf16 = jnp.bfloat16
    own = pltpu.VMEM((rows, width), bf16)
    caches = pltpu.VMEM(cached_key_rows.shape, bf16)
    messages = pltpu.VMEM((PLANE, 16, width // 2), bf16)
    lines = pltpu.VMEM((SIDE, rows, width), bf16)
    parts = len(PARTS)
    both = pl.pallas_call(
        kernel,
        out_shape=jax.ShapeDtypeStruct((2, rows, width), bf16),
        in_specs=[hbm] * 14,
        out_specs=vmem,
        scratch_shapes=[
            own,
            caches,
            caches,
            own,
            pltpu.VMEM(new_key_value.shape, bf16),
            pltpu.VMEM((1, rows), jnp.int32),
            pltpu.VMEM((1, 128), jnp.float32),
            pltpu.VMEM((1, 128), jnp.float32),
            pltpu.VMEM((1, width), jnp.float32),
            pltpu.VMEM((expert_ids.shape[1], rows), jnp.int32),
            pltpu.VMEM((expert_ids.shape[1], rows), jnp.float32),
            pltpu.VMEM((2, 256, slots), jnp.float32),
            pltpu.VMEM((256, 128), jnp.float32),
            own,
            pltpu.VMEM((width, 256), bf16),
            pltpu.VMEM((SIDE, SIDE, rows, width), bf16),
            pltpu.VMEM((SIDE, SIDE, rows, 256), bf16),
            own,
            own,
            pltpu.VMEM((width, 2 * hidden), bf16),
            pltpu.VMEM((hidden, width), bf16),
            pltpu.VMEM((3, SIDE, rows, 256), bf16),
            lines,
            messages,
            messages,
            pltpu.VMEM((256, width), bf16),
            pltpu.VMEM((256, 2 * hidden), jnp.float32),
            messages,
            messages,
            lines,
            lines,
            pltpu.VMEM((3, 256, SIDE * rows), bf16),
            pltpu.VMEM((3, 2 * SIDE * rows, 512), bf16),
            pltpu.VMEM((3, 256, 256), bf16),
            pltpu.VMEM((3, 256, 256), bf16),
            sems((11,)),
            sems((3,)),
            sems((2, SIDE)),
            sems((2, SIDE)),
            sems((2, SIDE, SIDE)),
            sems((2, SIDE, SIDE)),
            sems((2, SIDE)),
            sems((SIDE, SIDE)),
            sems((SIDE, SIDE)),
            sems((3 + 6 * parts,)),
            sems((3, SIDE)),
            sems((3, SIDE)),
            sems((3, SIDE)),
            sems((3, SIDE)),
            sems((parts, 3)),
            sems((parts, 3)),
            sems((parts, 3)),
            sems((parts, 3)),
            sems((3, SIDE)),
            sems((3, SIDE)),
        ],
        compiler_params=pltpu.CompilerParams(
            collective_id=1, has_side_effects=True, vmem_limit_bytes=60 << 20
        ),
        name="layer",
    )(
        residual, query, new_key_value, cached_key_rows, cached_value_rows,
        lengths.reshape(1, rows), q_gain.reshape(1, 128), k_gain.reshape(1, 128), out_weight,
        moe_gain.reshape(1, width), expert_ids.T, gate_probs.T, expert_gate_up, expert_down,
    )
    return (both[0], both[1])


def solution(mesh):
    return jax.shard_map(
        local,
        mesh=mesh,
        in_specs=(
            P(("dp", "ep"), None),
            P(("dp", "ep"), None),
            P(("dp", "ep"), None, None),
            P(("dp", "ep"), None, None),
            P(("dp", "ep"), None, None),
            P(("dp", "ep")),
            P(),
            P(),
            P(None, "ep"),
            P(),
            P(("dp", "ep"), None),
            P(("dp", "ep"), None),
            P(("dp", "ep"), None, None),
            P(("dp", "ep"), None, None),
        ),
        out_specs=(P(("dp", "ep"), None), P(("dp", "ep"), None)),
        check_vma=False,
    )
```

```python
import math

import jax
import jax.numpy as jnp
from jax import lax
from jax.experimental import pallas as pl
from jax.experimental.pallas import tpu as pltpu
from jax.sharding import PartitionSpec as P

EPSILON = 1e-06
THETA = 1000000.0


MESH = pl.DeviceIdType.MESH
SIDE = 4
PLANE = 2 * SIDE * SIDE
GROUPS = ((0, 1280), (1280, 1536), (2816, 1280))
PARTS = (
    ((0, 256), (0, 256), (0, 256)),
    ((256, 256), (256, 256), (256, 256)),
    ((512, 128), (512, 256), (512, 128)),
)


def place():
    y = lax.axis_index("dp")
    e = lax.axis_index("ep")
    return (e // 2) % SIDE, y, e // (2 * SIDE), e % 2


def device(x, y, z, core):
    return (y, (z * SIDE + x) * 2 + core)


def signal(target):
    pl.semaphore_signal(
        pltpu.get_barrier_semaphore(), inc=1, device_id=target, device_id_type=MESH
    )


def send(source, target, send_sem, recv_sem, where):
    pltpu.make_async_remote_copy(
        src_ref=source,
        dst_ref=target,
        send_sem=send_sem,
        recv_sem=recv_sem,
        device_id=where,
        device_id_type=MESH,
    ).start()


def wait(ref, sem):
    pltpu.make_async_copy(ref, ref, sem).wait()


def loop(first, last, body):
    def step(i, carry):
        body(i)
        return carry

    lax.fori_loop(first, last, step, 0)


def near_first(i):
    return 1 + 2 * i - 3 * (i // 2)


def route(ids, probs):
    top, count = ids.shape
    experts = 128
    weights = probs / jnp.sum(probs, axis=0, keepdims=True)
    label = iota((experts, count), 0)
    named = jnp.zeros((experts, count), jnp.float32)
    value = jnp.zeros((experts, count), jnp.float32)
    for k in range(top):
        match = ids[k : k + 1] == label
        named = named + jnp.where(match, 1.0, 0.0)
        value = value + jnp.where(match, weights[k : k + 1], 0.0)
    before = jnp.where(iota((count, count), 0) < iota((count, count), 1), 1.0, 0.0)
    earlier = jnp.dot(named, before, preferred_element_type=jnp.float32)
    again = earlier > 0.5
    both = jnp.concatenate(
        [jnp.where(again, 0.0, value), jnp.where(again, value, 0.0)], axis=0
    )
    return both.T.astype(jnp.bfloat16)


def turned(rows, cosines, sines, gain):
    mean_square = jnp.mean(rows * rows, axis=-1, keepdims=True)
    scaled = rows * lax.rsqrt(mean_square + EPSILON) * gain
    return (scaled * cosines + pltpu.roll(scaled, 64, 1) * sines).astype(jnp.bfloat16)


def halves(rows):
    width = rows.shape[1] // 2
    parts = rows.reshape(PLANE, 8, 2 * width)
    return jnp.concatenate([parts[:, :, :width], parts[:, :, width:]], axis=1).astype(jnp.bfloat16)


def iota(shape, dim):
    return lax.broadcasted_iota(jnp.int32, shape, dim)


def shifted(value, by, size):
    return (value >> by) & (size - 1)


def spot(axis, a, b, f):
    return ((f, a, b), (b, f, a), (b, a, f))[axis]


def ordered(axis, p, f, slot):
    x, y, z = spot(axis, shifted(p, 3, SIDE), shifted(p, 1, SIDE), f)
    return ((y * SIDE + z) * SIDE + x) * 4 + (p & 1) * 2 + slot


def ones_where(condition):
    return jnp.where(condition, 1.0, 0.0).astype(jnp.bfloat16)


def kernel(
    residual_in, query_in, new_in, keys_in, values_in, lengths_in, q_gain_in, k_gain_in, weight, moe_gain_in,
    ids_in, probs_in, gate_up, down, out,
    query, keys, values, residual, new, lengths, q_gain, k_gain, moe_gain, ids, probs, scores, products_pv, heads, columns_held, blocks, products, projected,
    normed, gate_up_held, down_held, meta, shared, picked, received, ordered_rows, total, answers, returned,
    partial, landed, choose, weigh, gather, spread,
    cache_sems, head_weight_sems, first_send, first_recv, second_send, second_recv, relay_send, back_send, back_recv,
    weight_sems, meta_send, meta_recv, share_send, share_recv, out_send, out_recv,
    ret_send, ret_recv, sum_send, sum_recv,
):
    attended, mixed = out.at[0], out.at[1]
    x, y, z, core = place()
    along = (x, y, z)
    across = ((y, z), (z, x), (y, x))
    axes = range(3)
    index = [(a * SIDE + b) * 2 + core for a, b in across]

    def on_line(axis, f):
        return device(*[f if i == axis else along[i] for i in axes], core)

    def in_plane(axis, p):
        return device(*spot(axis, p // (2 * SIDE), (p // 2) % SIDE, along[axis]), p % 2)

    def partner(axis, i):
        step = (27 * i) % PLANE
        a, b = across[axis]
        return (((a + step // (2 * SIDE)) % SIDE) * SIDE + (b + step // 2) % SIDE) * 2 + (core + step) % 2

    def each_partner(body):
        def one(i):
            for axis in axes:
                body(axis, partner(axis, i))

        loop(1, PLANE, one)

    def columns(axis):
        return pl.ds(*GROUPS[axis])

    def lanes(part, axis):
        start, size = PARTS[part][axis]
        return pl.ds(GROUPS[axis][0] // 2 + start, size)

    def both_columns(part, axis):
        start, size = PARTS[part][axis]
        base, width = GROUPS[axis]
        return pl.ds(base + start, size), pl.ds(base + width // 2 + start, size)

    loads = [
        pltpu.make_async_copy(source, target, cache_sems.at[i])
        for i, (source, target) in enumerate(
            (
                (query_in, query), (keys_in, keys), (values_in, values), (residual_in, residual),
                (new_in, new), (lengths_in, lengths), (q_gain_in, q_gain), (k_gain_in, k_gain),
                (moe_gain_in, moe_gain), (ids_in, ids), (probs_in, probs),
            )
        )
    ]
    for i in (0, 4, 5, 6, 7, 1, 2, 9, 10, 8, 3):
        loads[i].start()
    half = pl.ds(pl.multiple_of(core * 128, 128), 128)
    own_weight = pltpu.make_async_copy(weight, columns_held.at[:, half], head_weight_sems.at[0])
    own_weight.start()
    def greet(i):
        signal(device((x + i) % SIDE, y, z, core))
        signal(device(x, y, (z + i) % SIDE, core))
        signal(device(x, (y + i) % SIDE, z, core))
        signal(device(x, (y + i) % SIDE, z, 1 - core))

    signal(device(x, y, z, 1 - core))
    loop(1, SIDE, greet)
    order, place_of = [], {}
    for part in range(len(PARTS)):
        for axis in axes:
            for h, cols in enumerate(both_columns(part, axis)):
                place_of[part, axis, h] = pl.ds(sum(c.size for c in order), cols.size)
                order.append(cols)
    gate_up_fetches = [
        pltpu.make_async_copy(gate_up.at[0, cols], gate_up_held.at[to], weight_sems.at[3 + i])
        for i, (cols, to) in enumerate(zip(order, place_of.values()))
    ]
    fetches = gate_up_fetches + [
        pltpu.make_async_copy(down.at[0, :, cols], down_held.at[:, cols], weight_sems.at[i])
        for i, cols in enumerate([pl.ds(*group) for group in GROUPS])
    ]
    for fetch in fetches:
        fetch.start()
    for load in loads[4:8]:
        load.wait()
    tokens, slots, group = 16, keys.shape[1], 16
    pairs = tokens * group
    nt = (((1,), (1,)), ((), ()))

    def exact(left, right, dims=(((1,), (0,)), ((), ()))):
        return lax.dot_general(left, right, dims, preferred_element_type=jnp.float32)

    count = jnp.broadcast_to(lengths[...].astype(jnp.float32), (128, tokens)).astype(jnp.bfloat16)
    same_token = ones_where(iota((pairs, tokens), 0) >> 4 == iota((pairs, tokens), 1))
    eye = ones_where(iota((tokens, tokens), 0) == iota((tokens, tokens), 1))
    position = exact(eye, count, nt)
    lane = iota((tokens, 128), 1)
    freqs = jnp.exp((lane & 63).astype(jnp.float32) * (-2.0 * math.log(THETA) / 128))
    angles = position * freqs
    cosines = jnp.cos(angles)
    sines = jnp.where(lane < 64, -1.0, 1.0) * jnp.sin(angles)
    row, col = iota((pairs, pairs), 0), iota((pairs, pairs), 1)
    swap = ones_where(((row >> 4) == (col & 15)) & ((row & 15) == (col >> 4)))
    live = iota((pairs, slots), 1) < jnp.concatenate(
        [exact(same_token, count, nt)] * (slots // 128), axis=1
    ).astype(jnp.int32)
    scale = 1.0 / math.sqrt(128)
    many_cosines = jnp.concatenate([cosines] * group, axis=0)
    many_sines = jnp.concatenate([sines] * group, axis=0)
    loads[0].wait()

    def score(kv):
        stack = jnp.concatenate(
            [query[:, (kv * group + h) * 128 : (kv * group + h + 1) * 128] for h in range(group)], axis=0
        ).astype(jnp.float32)
        rotated = exact(swap, turned(stack, many_cosines, many_sines, q_gain[...]))
        new_key = turned(
            new[:, 0, kv * 128 : kv * 128 + 128].astype(jnp.float32), cosines, sines, k_gain[...]
        )
        own = jnp.sum(rotated * exact(same_token, new_key), axis=-1, keepdims=True) * scale
        queries = rotated.astype(jnp.bfloat16)
        if kv == 0:
            loads[1].wait()
        for t in range(tokens):
            scores[kv, t * group : (t + 1) * group] = exact(
                queries[t * group : (t + 1) * group], keys[t, :, kv * 128 : kv * 128 + 128], nt
            )
        return own

    def attend(kv):
        lanes_of = slice(kv * 128, kv * 128 + 128)
        own = score(kv)
        masked = jnp.where(live, scores[kv] * scale, -jnp.inf)
        highest = jnp.maximum(jnp.max(masked, axis=-1, keepdims=True), own)
        expos = jnp.exp(masked - highest)
        own_expo = jnp.exp(own - highest)
        sums = jnp.sum(expos, axis=-1, keepdims=True) + own_expo
        probs_of = (expos / sums).astype(jnp.bfloat16)
        own_prob = (own_expo / sums).astype(jnp.bfloat16).astype(jnp.float32)
        if kv == 0:
            loads[2].wait()
        for t in range(tokens):
            products_pv[t * group : (t + 1) * group] = exact(
                probs_of[t * group : (t + 1) * group], values[t, :, lanes_of]
            )
        new_value = exact(same_token, new[:, 1, kv * 128 : kv * 128 + 128])
        result = (products_pv[...] + own_prob * new_value).astype(jnp.bfloat16)
        result = exact(swap, result).astype(jnp.bfloat16)
        for h in range(group):
            heads[:, (kv * group + h) * 128 : (kv * group + h + 1) * 128] = result[
                h * tokens : (h + 1) * tokens
            ]

    first = x * (1 - core) + z * core
    second = z * (1 - core) + x * core

    def at(f, s):
        return device(f * (1 - core) + s * core, y, s * (1 - core) + f * core, core)

    width = heads.shape[1]
    wide = width // 2

    def side(kv):
        return pl.ds(kv * wide, wide)

    def start_first(kv):
        def one(i):
            f = (first + near_first(i)) % SIDE
            send(
                heads.at[:, side(kv)], blocks.at[second, first, :, side(kv)],
                first_send.at[kv, f], first_recv.at[kv, first], at(f, second),
            )

        loop(0, SIDE - 1, one)

    def start_second(kv, f, source):
        def one(i):
            s = (second + near_first(i)) % SIDE
            send(
                source, blocks.at[second, f, :, side(kv)], second_send.at[kv, s, f],
                second_recv.at[kv, second, f], at(first, s),
            )

        loop(0, 2, one)

    sibling = device(x, y, z, 1 - core)
    attend(0)
    pl.semaphore_wait(pltpu.get_barrier_semaphore(), 1 + 4 * (SIDE - 1))
    start_first(0)
    start_second(0, first, heads.at[:, side(0)])
    attend(1)
    start_first(1)
    start_second(1, first, heads.at[:, side(1)])
    send(weight, columns_held.at[:, half], head_weight_sems.at[1], head_weight_sems.at[2], sibling)

    loads[9].wait()
    loads[10].wait()
    own_meta = route(ids[...], probs[...])
    for axis in axes:
        meta[axis, along[axis]] = own_meta

    def to_line(axis, body):
        def one(i):
            body((along[axis] + near_first(i)) % SIDE)

        loop(0, SIDE - 1, one)

    for axis in axes:
        own = along[axis]
        to_line(axis, lambda f: send(
            meta.at[axis, own], meta.at[axis, own], meta_send.at[axis, f], meta_recv.at[axis, own],
            on_line(axis, f),
        ))
    blocks[second, first] = heads[...]
    for kv in range(2):
        def pass_on(i):
            f = (first + near_first(i)) % SIDE
            wait(blocks.at[second, f, :, side(kv)], first_recv.at[kv, f])
            start_second(kv, f, blocks.at[second, f, :, side(kv)])

        loop(0, SIDE - 1, pass_on)
    before, after = (second + SIDE - 1) % SIDE, (second + 1) % SIDE

    def relay(kv, f):
        origin, to = ((before, after), (after, before))[kv]
        piece = blocks.at[origin, f, :, side(kv)]
        wait(piece, second_recv.at[kv, origin, f])
        send(piece, piece, relay_send.at[kv, f], second_recv.at[kv, origin, f], at(first, to))

    for kv in range(2):
        relay(kv, first)
    for kv in range(2):
        loop(0, SIDE - 1, lambda i: relay(kv, (first + near_first(i)) % SIDE))
    own_weight.wait()
    wait(weight, head_weight_sems.at[2])
    mine = pl.ds(pl.multiple_of((z * SIDE + x) * 256, 256), 256)

    def project(s):
        rows = blocks[s].reshape(SIDE * tokens, width)
        products[s] = exact(rows, columns_held[...]).astype(jnp.bfloat16).reshape(SIDE, tokens, 256)

    def back(f, s):
        send(
            products.at[s, f], projected.at[:, mine], back_send.at[s, f],
            back_recv.at[second, first], at(f, s),
        )

    project(second)
    projected[:, mine] = products[second, first]
    loop(0, SIDE - 1, lambda i: back((first + near_first(i)) % SIDE, second))

    for axis in axes:
        q = iota((1, 256), 1)
        target = ordered(axis, q >> 3, shifted(q, 1, SIDE), q & 1)
        gather[axis] = ones_where(iota((256, 256), 0) == target)
        q = iota((256, 1), 0)
        target = ordered(axis, q >> 3, shifted(q, 1, SIDE), q & 1)
        spread[axis] = ones_where(iota((256, 256), 1) == target)

    for axis in axes:
        to_line(axis, lambda f: wait(meta.at[axis, 0], meta_recv.at[axis, f]))
        known = meta[axis].reshape(SIDE * 16, 256)
        present = ones_where(known.astype(jnp.float32) > 0.0)

        def expert(p):
            ex, ey, ez = spot(axis, shifted(p, 3, SIDE), shifted(p, 1, SIDE), along[axis])
            return (ey * SIDE + ez) * (2 * SIDE) + ex * 2 + (p & 1)

        q = iota((256, 1), 0)
        wanted = ones_where(iota((256, 256), 1) == (q & 1) * 128 + expert(q >> 3))
        chosen = lax.dot_general(wanted, present, nt, preferred_element_type=jnp.float32)
        same = shifted(q, 1, SIDE) == iota((1, SIDE * 16), 1) >> 4
        choose[axis] = jnp.where(same, chosen, 0.0).astype(jnp.bfloat16)
        q = iota((512, 1), 0)
        wanted = ones_where(iota((512, 256), 1) == (q & 1) * 128 + expert(q >> 4))
        scaled = lax.dot_general(known, wanted, nt, preferred_element_type=jnp.float32)
        q = iota((1, 512), 1)
        scaled = jnp.where(iota((SIDE * 16, 1), 0) >> 4 == shifted(q, 1, SIDE), scaled, 0.0)
        upper = shifted(q, 3, 2) == 0
        weigh[axis] = jnp.concatenate(
            [jnp.where(upper, scaled, 0.0), jnp.where(upper, 0.0, scaled)], axis=0
        ).astype(jnp.bfloat16)

    def group_of(s, halves_left):
        for kv in halves_left:
            loop(0, SIDE, lambda f: wait(blocks.at[s, f, :, side(kv)], second_recv.at[kv, s, f]))
        project(s)
        loop(0, SIDE, lambda f: back(f, s))

    group_of(before, (1,))
    group_of(after, (0,))
    group_of((second + 2) % SIDE, (0, 1))

    def others_in_plane(body):
        def one(i):
            other = (second * SIDE + first + i) % (SIDE * SIDE)
            body(other % SIDE, other // SIDE)

        loop(1, SIDE * SIDE, one)

    others_in_plane(lambda f, s: wait(products.at[s, f], back_recv.at[s, f]))
    loads[3].wait()
    loads[8].wait()
    added = residual[...].astype(jnp.float32) + projected[...].astype(jnp.float32)
    rounded = added.astype(jnp.bfloat16)
    attended[...] = rounded
    stream = rounded.astype(jnp.float32)
    level = lax.rsqrt(jnp.mean(stream * stream, axis=-1, keepdims=True) + EPSILON)
    normed[...] = (stream * level * moe_gain[...]).astype(jnp.bfloat16)
    for axis in axes:
        own = along[axis]
        to_line(axis, lambda f: send(
            normed.at[:, columns(axis)], shared.at[own, :, columns(axis)],
            share_send.at[axis, f], share_recv.at[axis, own], on_line(axis, f),
        ))
        shared[along[axis], :, columns(axis)] = normed[:, columns(axis)]

    def dispatch(part, axis):
        loop(1, PLANE, lambda i: send(
            picked.at[partner(axis, i), :, lanes(part, axis)], received.at[index[axis], :, lanes(part, axis)],
            out_send.at[part, axis], out_recv.at[part, axis], in_plane(axis, partner(axis, i)),
        ))

    for axis in axes:
        to_line(axis, lambda f: wait(shared.at[0, :, columns(axis)], share_recv.at[axis, f]))
        rows = shared[:, :, columns(axis)].reshape(SIDE * 16, GROUPS[axis][1])
        result = jnp.dot(choose[axis], rows, preferred_element_type=jnp.float32)
        base, width = GROUPS[axis]
        picked[:, :, pl.ds(base // 2, width // 2)] = halves(result)
        dispatch(0, axis)
    for part in range(1, len(PARTS)):
        each_partner(lambda axis, p: send(
            picked.at[p, :, lanes(part, axis)], received.at[index[axis], :, lanes(part, axis)],
            out_send.at[part, axis], out_recv.at[part, axis], in_plane(axis, p),
        ))
    for axis in axes:
        base, width = GROUPS[axis]
        whole = pl.ds(base // 2, width // 2)
        received[index[axis], :, whole] = picked[index[axis], :, whole]

    hidden_size = down.shape[1]
    many = pl.ds(0, PLANE - 1)
    for part in range(len(PARTS)):
        for axis in axes:
            wait(received.at[many, :, lanes(part, axis)], out_recv.at[part, axis])
            size = PARTS[part][axis][1]
            messages = received[:, :, lanes(part, axis)].astype(jnp.float32)
            for h in range(2):
                rows = messages[:, h * 8 : h * 8 + 8].reshape(PLANE * 8, size).astype(jnp.bfloat16)
                rows = jnp.dot(gather[axis], rows, preferred_element_type=jnp.float32)
                ordered_rows[:, place_of[part, axis, h]] = rows.astype(jnp.bfloat16)
        for fetch in gate_up_fetches[6 * part : 6 * part + 6]:
            fetch.wait()
        start = place_of[part, 0, 0].start
        depth = pl.ds(start, 2 * sum(p[1] for p in PARTS[part]))

        def step(n):
            piece = pl.ds(pl.multiple_of(n * 768, 768), 768)
            product = jnp.dot(
                ordered_rows[:, depth], gate_up_held[depth, piece], preferred_element_type=jnp.float32
            )
            if part == 0:
                total[:, piece] = product
            else:
                total[:, piece] += product

        loop(0, 2 * hidden_size // 768, step)

    gate = total[:, :hidden_size]
    hidden = (gate / (1.0 + jnp.exp(-gate)) * total[:, hidden_size:]).astype(jnp.bfloat16)
    for axis in axes:
        fetches[len(order) + axis].wait()
    hiddens = [
        jnp.dot(spread[axis], hidden, preferred_element_type=jnp.float32).astype(jnp.bfloat16)
        for axis in axes
    ]
    for part in range(len(PARTS)):
        for axis in axes:
            upper, lower = both_columns(part, axis)
            result = [
                jnp.dot(hiddens[axis], down_held[:, cols], preferred_element_type=jnp.float32)
                for cols in (upper, lower)
            ]
            answers[:, :, lanes(part, axis)] = halves(jnp.concatenate(result, axis=1))
        each_partner(lambda axis, p: send(
            answers.at[p, :, lanes(part, axis)], returned.at[index[axis], :, lanes(part, axis)],
            ret_send.at[part, axis], ret_recv.at[part, axis], in_plane(axis, p),
        ))
        for axis in axes:
            returned[index[axis], :, lanes(part, axis)] = answers[index[axis], :, lanes(part, axis)]

    for part in range(len(PARTS)):
        for axis in axes:
            wait(returned.at[many, :, lanes(part, axis)], ret_recv.at[part, axis])
            size = PARTS[part][axis][1]
            messages = returned[:, :, lanes(part, axis)].reshape(PLANE * 16, size)
            result = jnp.dot(weigh[axis], messages, preferred_element_type=jnp.float32)
            result = result.astype(jnp.bfloat16).reshape(2, SIDE, 16, size)
            upper, lower = both_columns(part, axis)
            partial[:, :, upper] = result[0]
            partial[:, :, lower] = result[1]
            if part == len(PARTS) - 1:
                own = along[axis]
                to_line(axis, lambda f: send(
                    partial.at[f, :, columns(axis)], landed.at[own, :, columns(axis)],
                    sum_send.at[axis, f], sum_recv.at[axis, own], on_line(axis, f),
                ))
    for axis in axes:
        to_line(axis, lambda f: wait(landed.at[0, :, columns(axis)], sum_recv.at[axis, f]))
        own = along[axis]
        block = partial[own, :, columns(axis)].astype(jnp.float32)
        for d in range(1, SIDE):
            block = block + landed[(own + d) % SIDE, :, columns(axis)].astype(jnp.float32)
        block = block + attended[:, columns(axis)].astype(jnp.float32)
        mixed[:, columns(axis)] = block.astype(jnp.bfloat16)

    wait(weight, head_weight_sems.at[1])
    for kv in range(2):
        loop(1, SIDE, lambda i: wait(heads.at[:, side(kv)], first_send.at[kv, (first + i) % SIDE]))
        for s in (before, after):
            loop(0, SIDE, lambda g: wait(heads.at[:, side(kv)], second_send.at[kv, s, g]))
        loop(0, SIDE, lambda g: wait(heads.at[:, side(kv)], relay_send.at[kv, g]))
    others_in_plane(lambda f, s: wait(products.at[s, f], back_send.at[s, f]))
    for axis in axes:
        to_line(axis, lambda f: wait(meta.at[axis, 0], meta_send.at[axis, f]))
        to_line(axis, lambda f: wait(landed.at[0, :, columns(axis)], share_send.at[axis, f]))
        to_line(axis, lambda f: wait(landed.at[0, :, columns(axis)], sum_send.at[axis, f]))
        for part in range(len(PARTS)):
            wait(picked.at[many, :, lanes(part, axis)], out_send.at[part, axis])
            wait(answers.at[many, :, lanes(part, axis)], ret_send.at[part, axis])


def local(
    residual,
    query,
    new_key_value,
    cached_key_rows,
    cached_value_rows,
    lengths,
    q_gain,
    k_gain,
    out_weight,
    moe_gain,
    expert_ids,
    gate_probs,
    expert_gate_up,
    expert_down,
):
    rows, width = residual.shape
    hidden = expert_down.shape[1]
    slots = cached_key_rows.shape[1]
    vmem = pl.BlockSpec(memory_space=pltpu.VMEM)
    hbm = pl.BlockSpec(memory_space=pltpu.HBM)
    sems = pltpu.SemaphoreType.DMA
    bf16 = jnp.bfloat16
    own = pltpu.VMEM((rows, width), bf16)
    caches = pltpu.VMEM(cached_key_rows.shape, bf16)
    messages = pltpu.VMEM((PLANE, 16, width // 2), bf16)
    lines = pltpu.VMEM((SIDE, rows, width), bf16)
    parts = len(PARTS)
    both = pl.pallas_call(
        kernel,
        out_shape=jax.ShapeDtypeStruct((2, rows, width), bf16),
        in_specs=[hbm] * 14,
        out_specs=vmem,
        scratch_shapes=[
            own,
            caches,
            caches,
            own,
            pltpu.VMEM(new_key_value.shape, bf16),
            pltpu.VMEM((1, rows), jnp.int32),
            pltpu.VMEM((1, 128), jnp.float32),
            pltpu.VMEM((1, 128), jnp.float32),
            pltpu.VMEM((1, width), jnp.float32),
            pltpu.VMEM((expert_ids.shape[1], rows), jnp.int32),
            pltpu.VMEM((expert_ids.shape[1], rows), jnp.float32),
            pltpu.VMEM((2, 256, slots), jnp.float32),
            pltpu.VMEM((256, 128), jnp.float32),
            own,
            pltpu.VMEM((width, 256), bf16),
            pltpu.VMEM((SIDE, SIDE, rows, width), bf16),
            pltpu.VMEM((SIDE, SIDE, rows, 256), bf16),
            own,
            own,
            pltpu.VMEM((width, 2 * hidden), bf16),
            pltpu.VMEM((hidden, width), bf16),
            pltpu.VMEM((3, SIDE, rows, 256), bf16),
            lines,
            messages,
            messages,
            pltpu.VMEM((256, width), bf16),
            pltpu.VMEM((256, 2 * hidden), jnp.float32),
            messages,
            messages,
            lines,
            lines,
            pltpu.VMEM((3, 256, SIDE * rows), bf16),
            pltpu.VMEM((3, 2 * SIDE * rows, 512), bf16),
            pltpu.VMEM((3, 256, 256), bf16),
            pltpu.VMEM((3, 256, 256), bf16),
            sems((11,)),
            sems((3,)),
            sems((2, SIDE)),
            sems((2, SIDE)),
            sems((2, SIDE, SIDE)),
            sems((2, SIDE, SIDE)),
            sems((2, SIDE)),
            sems((SIDE, SIDE)),
            sems((SIDE, SIDE)),
            sems((3 + 6 * parts,)),
            sems((3, SIDE)),
            sems((3, SIDE)),
            sems((3, SIDE)),
            sems((3, SIDE)),
            sems((parts, 3)),
            sems((parts, 3)),
            sems((parts, 3)),
            sems((parts, 3)),
            sems((3, SIDE)),
            sems((3, SIDE)),
        ],
        compiler_params=pltpu.CompilerParams(
            collective_id=1, has_side_effects=True, vmem_limit_bytes=60 << 20
        ),
        name="layer",
    )(
        residual, query, new_key_value, cached_key_rows, cached_value_rows,
        lengths.reshape(1, rows), q_gain.reshape(1, 128), k_gain.reshape(1, 128), out_weight,
        moe_gain.reshape(1, width), expert_ids.T, gate_probs.T, expert_gate_up, expert_down,
    )
    return (both[0], both[1])


def solution(mesh):
    return jax.shard_map(
        local,
        mesh=mesh,
        in_specs=(
            P(("dp", "ep"), None),
            P(("dp", "ep"), None),
            P(("dp", "ep"), None, None),
            P(("dp", "ep"), None, None),
            P(("dp", "ep"), None, None),
            P(("dp", "ep")),
            P(),
            P(),
            P(None, "ep"),
            P(),
            P(("dp", "ep"), None),
            P(("dp", "ep"), None),
            P(("dp", "ep"), None, None),
            P(("dp", "ep"), None, None),
        ),
        out_specs=(P(("dp", "ep"), None), P(("dp", "ep"), None)),
        check_vma=False,
    )
```

```python
import math

import jax
import jax.numpy as jnp
from jax import lax
from jax.experimental import pallas as pl
from jax.experimental.pallas import tpu as pltpu
from jax.sharding import PartitionSpec as P

EPSILON = 1e-06
THETA = 1000000.0


MESH = pl.DeviceIdType.MESH
SIDE = 4
PLANE = 2 * SIDE * SIDE
GROUPS = ((0, 1280), (1280, 1536), (2816, 1280))
PARTS = (
    ((0, 256), (0, 256), (0, 256)),
    ((256, 256), (256, 256), (256, 256)),
    ((512, 128), (512, 256), (512, 128)),
)


def place():
    y = lax.axis_index("dp")
    e = lax.axis_index("ep")
    return (e // 2) % SIDE, y, e // (2 * SIDE), e % 2


def device(x, y, z, core):
    return (y, (z * SIDE + x) * 2 + core)


def signal(target):
    pl.semaphore_signal(
        pltpu.get_barrier_semaphore(), inc=1, device_id=target, device_id_type=MESH
    )


def send(source, target, send_sem, recv_sem, where):
    pltpu.make_async_remote_copy(
        src_ref=source,
        dst_ref=target,
        send_sem=send_sem,
        recv_sem=recv_sem,
        device_id=where,
        device_id_type=MESH,
    ).start()


def wait(ref, sem):
    pltpu.make_async_copy(ref, ref, sem).wait()


def loop(first, last, body):
    def step(i, carry):
        body(i)
        return carry

    lax.fori_loop(first, last, step, 0)


def near_first(i):
    return 1 + 2 * i - 3 * (i // 2)


def route(ids, probs):
    top, count = ids.shape
    experts = 128
    weights = probs / jnp.sum(probs, axis=0, keepdims=True)
    label = iota((experts, count), 0)
    named = jnp.zeros((experts, count), jnp.float32)
    value = jnp.zeros((experts, count), jnp.float32)
    for k in range(top):
        match = ids[k : k + 1] == label
        named = named + jnp.where(match, 1.0, 0.0)
        value = value + jnp.where(match, weights[k : k + 1], 0.0)
    before = jnp.where(iota((count, count), 0) < iota((count, count), 1), 1.0, 0.0)
    earlier = jnp.dot(named, before, preferred_element_type=jnp.float32)
    again = earlier > 0.5
    both = jnp.concatenate(
        [jnp.where(again, 0.0, value), jnp.where(again, value, 0.0)], axis=0
    )
    return both.T.astype(jnp.bfloat16)


def turned(rows, cosines, sines, gain):
    mean_square = jnp.mean(rows * rows, axis=-1, keepdims=True)
    scaled = rows * lax.rsqrt(mean_square + EPSILON) * gain
    return (scaled * cosines + pltpu.roll(scaled, 64, 1) * sines).astype(jnp.bfloat16)


def halves(rows):
    width = rows.shape[1] // 2
    parts = rows.reshape(PLANE, 8, 2 * width)
    return jnp.concatenate([parts[:, :, :width], parts[:, :, width:]], axis=1).astype(jnp.bfloat16)


def iota(shape, dim):
    return lax.broadcasted_iota(jnp.int32, shape, dim)


def shifted(value, by, size):
    return (value >> by) & (size - 1)


def spot(axis, a, b, f):
    return ((f, a, b), (b, f, a), (b, a, f))[axis]


def ordered(axis, p, f, slot):
    x, y, z = spot(axis, shifted(p, 3, SIDE), shifted(p, 1, SIDE), f)
    return ((y * SIDE + z) * SIDE + x) * 4 + (p & 1) * 2 + slot


def ones_where(condition):
    return jnp.where(condition, 1.0, 0.0).astype(jnp.bfloat16)


def kernel(
    residual_in, query_in, new_in, keys_in, values_in, lengths_in, q_gain_in, k_gain_in, weight, moe_gain_in,
    ids_in, probs_in, gate_up, down, out,
    query, keys, values, residual, new, lengths, q_gain, k_gain, moe_gain, ids, probs, scores, products_pv, heads, columns_held, blocks, products, projected,
    normed, gate_up_held, down_held, meta, shared, picked, received, ordered_rows, total, answers, returned,
    partial, landed, choose, weigh, gather, spread,
    cache_sems, head_weight_sems, first_send, first_recv, second_send, second_recv, relay_send, back_send, back_recv,
    weight_sems, meta_send, meta_recv, share_send, share_recv, out_send, out_recv,
    ret_send, ret_recv, sum_send, sum_recv,
):
    attended, mixed = out.at[0], out.at[1]
    x, y, z, core = place()
    along = (x, y, z)
    across = ((y, z), (z, x), (y, x))
    axes = range(3)
    index = [(a * SIDE + b) * 2 + core for a, b in across]

    def on_line(axis, f):
        return device(*[f if i == axis else along[i] for i in axes], core)

    def in_plane(axis, p):
        return device(*spot(axis, p // (2 * SIDE), (p // 2) % SIDE, along[axis]), p % 2)

    def partner(axis, i):
        step = (27 * i) % PLANE
        a, b = across[axis]
        return (((a + step // (2 * SIDE)) % SIDE) * SIDE + (b + step // 2) % SIDE) * 2 + (core + step) % 2

    def each_partner(body):
        def one(i):
            for axis in axes:
                body(axis, partner(axis, i))

        loop(1, PLANE, one)

    def columns(axis):
        return pl.ds(*GROUPS[axis])

    def lanes(part, axis):
        start, size = PARTS[part][axis]
        return pl.ds(GROUPS[axis][0] // 2 + start, size)

    def both_columns(part, axis):
        start, size = PARTS[part][axis]
        base, width = GROUPS[axis]
        return pl.ds(base + start, size), pl.ds(base + width // 2 + start, size)

    loads = [
        pltpu.make_async_copy(source, target, cache_sems.at[i])
        for i, (source, target) in enumerate(
            (
                (query_in, query), (keys_in, keys), (values_in, values), (residual_in, residual),
                (new_in, new), (lengths_in, lengths), (q_gain_in, q_gain), (k_gain_in, k_gain),
                (moe_gain_in, moe_gain), (ids_in, ids), (probs_in, probs),
            )
        )
    ]
    for i in (0, 4, 5, 6, 7, 1, 2, 9, 10, 8, 3):
        loads[i].start()
    half = pl.ds(pl.multiple_of(core * 128, 128), 128)
    own_weight = pltpu.make_async_copy(weight, columns_held.at[:, half], head_weight_sems.at[0])
    own_weight.start()
    def greet(i):
        signal(device((x + i) % SIDE, y, z, core))
        signal(device(x, y, (z + i) % SIDE, core))
        signal(device(x, (y + i) % SIDE, z, core))
        signal(device(x, (y + i) % SIDE, z, 1 - core))

    signal(device(x, y, z, 1 - core))
    loop(1, SIDE, greet)
    order, place_of = [], {}
    for part in range(len(PARTS)):
        for axis in axes:
            for h, cols in enumerate(both_columns(part, axis)):
                place_of[part, axis, h] = pl.ds(sum(c.size for c in order), cols.size)
                order.append(cols)
    gate_up_fetches = [
        pltpu.make_async_copy(gate_up.at[0, cols], gate_up_held.at[to], weight_sems.at[3 + i])
        for i, (cols, to) in enumerate(zip(order, place_of.values()))
    ]
    fetches = gate_up_fetches + [
        pltpu.make_async_copy(down.at[0, :, cols], down_held.at[:, cols], weight_sems.at[i])
        for i, cols in enumerate([pl.ds(*group) for group in GROUPS])
    ]
    for fetch in fetches:
        fetch.start()
    for load in loads[4:8]:
        load.wait()
    tokens, slots, group = 16, keys.shape[1], 16
    pairs = tokens * group
    nt = (((1,), (1,)), ((), ()))

    def exact(left, right, dims=(((1,), (0,)), ((), ()))):
        return lax.dot_general(left, right, dims, preferred_element_type=jnp.float32)

    count = jnp.broadcast_to(lengths[...].astype(jnp.float32), (128, tokens)).astype(jnp.bfloat16)
    same_token = ones_where(iota((pairs, tokens), 0) >> 4 == iota((pairs, tokens), 1))
    eye = ones_where(iota((tokens, tokens), 0) == iota((tokens, tokens), 1))
    position = exact(eye, count, nt)
    lane = iota((tokens, 128), 1)
    freqs = jnp.exp((lane & 63).astype(jnp.float32) * (-2.0 * math.log(THETA) / 128))
    angles = position * freqs
    cosines = jnp.cos(angles)
    sines = jnp.where(lane < 64, -1.0, 1.0) * jnp.sin(angles)
    row, col = iota((pairs, pairs), 0), iota((pairs, pairs), 1)
    swap = ones_where(((row >> 4) == (col & 15)) & ((row & 15) == (col >> 4)))
    live = iota((pairs, slots), 1) < jnp.concatenate(
        [exact(same_token, count, nt)] * (slots // 128), axis=1
    ).astype(jnp.int32)
    scale = 1.0 / math.sqrt(128)
    many_cosines = jnp.concatenate([cosines] * group, axis=0)
    many_sines = jnp.concatenate([sines] * group, axis=0)
    loads[0].wait()

    def score(kv):
        stack = jnp.concatenate(
            [query[:, (kv * group + h) * 128 : (kv * group + h + 1) * 128] for h in range(group)], axis=0
        ).astype(jnp.float32)
        rotated = exact(swap, turned(stack, many_cosines, many_sines, q_gain[...]))
        new_key = turned(
            new[:, 0, kv * 128 : kv * 128 + 128].astype(jnp.float32), cosines, sines, k_gain[...]
        )
        own = jnp.sum(rotated * exact(same_token, new_key), axis=-1, keepdims=True) * scale
        queries = rotated.astype(jnp.bfloat16)
        if kv == 0:
            loads[1].wait()
        for t in range(tokens):
            scores[kv, t * group : (t + 1) * group] = exact(
                queries[t * group : (t + 1) * group], keys[t, :, kv * 128 : kv * 128 + 128], nt
            )
        return own

    def attend(kv):
        lanes_of = slice(kv * 128, kv * 128 + 128)
        own = score(kv)
        masked = jnp.where(live, scores[kv] * scale, -jnp.inf)
        highest = jnp.maximum(jnp.max(masked, axis=-1, keepdims=True), own)
        expos = jnp.exp(masked - highest)
        own_expo = jnp.exp(own - highest)
        sums = jnp.sum(expos, axis=-1, keepdims=True) + own_expo
        probs_of = (expos / sums).astype(jnp.bfloat16)
        own_prob = (own_expo / sums).astype(jnp.bfloat16).astype(jnp.float32)
        if kv == 0:
            loads[2].wait()
        for t in range(tokens):
            products_pv[t * group : (t + 1) * group] = exact(
                probs_of[t * group : (t + 1) * group], values[t, :, lanes_of]
            )
        new_value = exact(same_token, new[:, 1, kv * 128 : kv * 128 + 128])
        result = (products_pv[...] + own_prob * new_value).astype(jnp.bfloat16)
        result = exact(swap, result).astype(jnp.bfloat16)
        for h in range(group):
            heads[:, (kv * group + h) * 128 : (kv * group + h + 1) * 128] = result[
                h * tokens : (h + 1) * tokens
            ]

    first = x * (1 - core) + z * core
    second = z * (1 - core) + x * core

    def at(f, s):
        return device(f * (1 - core) + s * core, y, s * (1 - core) + f * core, core)

    width = heads.shape[1]
    wide = width // 2

    def side(kv):
        return pl.ds(kv * wide, wide)

    def start_first(kv):
        def one(i):
            f = (first + near_first(i)) % SIDE
            send(
                heads.at[:, side(kv)], blocks.at[second, first, :, side(kv)],
                first_send.at[kv, f], first_recv.at[kv, first], at(f, second),
            )

        loop(0, SIDE - 1, one)

    def start_second(kv, f, source):
        def one(i):
            s = (second + near_first(i)) % SIDE
            send(
                source, blocks.at[second, f, :, side(kv)], second_send.at[kv, s, f],
                second_recv.at[kv, second, f], at(first, s),
            )

        loop(0, 2, one)

    sibling = device(x, y, z, 1 - core)
    attend(0)
    pl.semaphore_wait(pltpu.get_barrier_semaphore(), 1 + 4 * (SIDE - 1))
    start_first(0)
    start_second(0, first, heads.at[:, side(0)])
    attend(1)
    start_first(1)
    start_second(1, first, heads.at[:, side(1)])
    send(weight, columns_held.at[:, half], head_weight_sems.at[1], head_weight_sems.at[2], sibling)

    loads[9].wait()
    loads[10].wait()
    own_meta = route(ids[...], probs[...])
    for axis in axes:
        meta[axis, along[axis]] = own_meta

    def to_line(axis, body):
        def one(i):
            body((along[axis] + near_first(i)) % SIDE)

        loop(0, SIDE - 1, one)

    for axis in axes:
        own = along[axis]
        to_line(axis, lambda f: send(
            meta.at[axis, own], meta.at[axis, own], meta_send.at[axis, f], meta_recv.at[axis, own],
            on_line(axis, f),
        ))
    blocks[second, first] = heads[...]
    for kv in range(2):
        def pass_on(i):
            f = (first + near_first(i)) % SIDE
            wait(blocks.at[second, f, :, side(kv)], first_recv.at[kv, f])
            start_second(kv, f, blocks.at[second, f, :, side(kv)])

        loop(0, SIDE - 1, pass_on)
    before, after = (second + SIDE - 1) % SIDE, (second + 1) % SIDE

    def relay(kv, f):
        origin, to = ((before, after), (after, before))[kv]
        piece = blocks.at[origin, f, :, side(kv)]
        wait(piece, second_recv.at[kv, origin, f])
        send(piece, piece, relay_send.at[kv, f], second_recv.at[kv, origin, f], at(first, to))

    for kv in range(2):
        relay(kv, first)
    for kv in range(2):
        loop(0, SIDE - 1, lambda i: relay(kv, (first + near_first(i)) % SIDE))
    own_weight.wait()
    wait(weight, head_weight_sems.at[2])
    mine = pl.ds(pl.multiple_of((z * SIDE + x) * 256, 256), 256)

    def project(s):
        rows = blocks[s].reshape(SIDE * tokens, width)
        products[s] = exact(rows, columns_held[...]).astype(jnp.bfloat16).reshape(SIDE, tokens, 256)

    def back(f, s):
        send(
            products.at[s, f], projected.at[:, mine], back_send.at[s, f],
            back_recv.at[second, first], at(f, s),
        )

    project(second)
    projected[:, mine] = products[second, first]
    loop(0, SIDE - 1, lambda i: back((first + near_first(i)) % SIDE, second))

    for axis in axes:
        q = iota((1, 256), 1)
        target = ordered(axis, q >> 3, shifted(q, 1, SIDE), q & 1)
        gather[axis] = ones_where(iota((256, 256), 0) == target)
        q = iota((256, 1), 0)
        target = ordered(axis, q >> 3, shifted(q, 1, SIDE), q & 1)
        spread[axis] = ones_where(iota((256, 256), 1) == target)

    for axis in axes:
        to_line(axis, lambda f: wait(meta.at[axis, 0], meta_recv.at[axis, f]))
        known = meta[axis].reshape(SIDE * 16, 256)
        present = ones_where(known.astype(jnp.float32) > 0.0)

        def expert(p):
            ex, ey, ez = spot(axis, shifted(p, 3, SIDE), shifted(p, 1, SIDE), along[axis])
            return (ey * SIDE + ez) * (2 * SIDE) + ex * 2 + (p & 1)

        q = iota((256, 1), 0)
        wanted = ones_where(iota((256, 256), 1) == (q & 1) * 128 + expert(q >> 3))
        chosen = lax.dot_general(wanted, present, nt, preferred_element_type=jnp.float32)
        same = shifted(q, 1, SIDE) == iota((1, SIDE * 16), 1) >> 4
        choose[axis] = jnp.where(same, chosen, 0.0).astype(jnp.bfloat16)
        q = iota((512, 1), 0)
        wanted = ones_where(iota((512, 256), 1) == (q & 1) * 128 + expert(q >> 4))
        scaled = lax.dot_general(known, wanted, nt, preferred_element_type=jnp.float32)
        q = iota((1, 512), 1)
        scaled = jnp.where(iota((SIDE * 16, 1), 0) >> 4 == shifted(q, 1, SIDE), scaled, 0.0)
        upper = shifted(q, 3, 2) == 0
        weigh[axis] = jnp.concatenate(
            [jnp.where(upper, scaled, 0.0), jnp.where(upper, 0.0, scaled)], axis=0
        ).astype(jnp.bfloat16)

    def group_of(s, halves_left):
        for kv in halves_left:
            loop(0, SIDE, lambda f: wait(blocks.at[s, f, :, side(kv)], second_recv.at[kv, s, f]))
        project(s)
        loop(0, SIDE, lambda f: back(f, s))

    group_of(before, (1,))
    group_of(after, (0,))
    group_of((second + 2) % SIDE, (0, 1))

    def others_in_plane(body):
        def one(i):
            other = (second * SIDE + first + i) % (SIDE * SIDE)
            body(other % SIDE, other // SIDE)

        loop(1, SIDE * SIDE, one)

    others_in_plane(lambda f, s: wait(products.at[s, f], back_recv.at[s, f]))
    loads[3].wait()
    loads[8].wait()
    added = residual[...].astype(jnp.float32) + projected[...].astype(jnp.float32)
    rounded = added.astype(jnp.bfloat16)
    attended[...] = rounded
    stream = rounded.astype(jnp.float32)
    level = lax.rsqrt(jnp.mean(stream * stream, axis=-1, keepdims=True) + EPSILON)
    normed[...] = (stream * level * moe_gain[...]).astype(jnp.bfloat16)
    for axis in axes:
        own = along[axis]
        to_line(axis, lambda f: send(
            normed.at[:, columns(axis)], shared.at[own, :, columns(axis)],
            share_send.at[axis, f], share_recv.at[axis, own], on_line(axis, f),
        ))
        shared[along[axis], :, columns(axis)] = normed[:, columns(axis)]

    def dispatch(part, axis):
        loop(1, PLANE, lambda i: send(
            picked.at[partner(axis, i), :, lanes(part, axis)], received.at[index[axis], :, lanes(part, axis)],
            out_send.at[part, axis], out_recv.at[part, axis], in_plane(axis, partner(axis, i)),
        ))

    for axis in axes:
        to_line(axis, lambda f: wait(shared.at[0, :, columns(axis)], share_recv.at[axis, f]))
        rows = shared[:, :, columns(axis)].reshape(SIDE * 16, GROUPS[axis][1])
        result = jnp.dot(choose[axis], rows, preferred_element_type=jnp.float32)
        base, width = GROUPS[axis]
        picked[:, :, pl.ds(base // 2, width // 2)] = halves(result)
        dispatch(0, axis)
    for part in range(1, len(PARTS)):
        each_partner(lambda axis, p: send(
            picked.at[p, :, lanes(part, axis)], received.at[index[axis], :, lanes(part, axis)],
            out_send.at[part, axis], out_recv.at[part, axis], in_plane(axis, p),
        ))
    for axis in axes:
        base, width = GROUPS[axis]
        whole = pl.ds(base // 2, width // 2)
        received[index[axis], :, whole] = picked[index[axis], :, whole]

    hidden_size = down.shape[1]
    many = pl.ds(0, PLANE - 1)
    for part in range(len(PARTS)):
        for axis in axes:
            wait(received.at[many, :, lanes(part, axis)], out_recv.at[part, axis])
            size = PARTS[part][axis][1]
            messages = received[:, :, lanes(part, axis)].astype(jnp.float32)
            for h in range(2):
                rows = messages[:, h * 8 : h * 8 + 8].reshape(PLANE * 8, size).astype(jnp.bfloat16)
                rows = jnp.dot(gather[axis], rows, preferred_element_type=jnp.float32)
                ordered_rows[:, place_of[part, axis, h]] = rows.astype(jnp.bfloat16)
        for fetch in gate_up_fetches[6 * part : 6 * part + 6]:
            fetch.wait()
        start = place_of[part, 0, 0].start
        depth = pl.ds(start, 2 * sum(p[1] for p in PARTS[part]))

        def step(n):
            piece = pl.ds(pl.multiple_of(n * 768, 768), 768)
            product = jnp.dot(
                ordered_rows[:, depth], gate_up_held[depth, piece], preferred_element_type=jnp.float32
            )
            if part == 0:
                total[:, piece] = product
            else:
                total[:, piece] += product

        if part < len(PARTS) - 1:
            loop(0, 2 * hidden_size // 768, step)

    gate, up = [
        total[:, piece]
        + jnp.dot(ordered_rows[:, depth], gate_up_held[depth, piece], preferred_element_type=jnp.float32)
        for piece in (pl.ds(0, hidden_size), pl.ds(hidden_size, hidden_size))
    ]
    hidden = (gate / (1.0 + jnp.exp(-gate)) * up).astype(jnp.bfloat16)
    for axis in axes:
        fetches[len(order) + axis].wait()
    hiddens = [
        jnp.dot(spread[axis], hidden, preferred_element_type=jnp.float32).astype(jnp.bfloat16)
        for axis in axes
    ]
    for part in range(len(PARTS)):
        for axis in axes:
            upper, lower = both_columns(part, axis)
            result = [
                jnp.dot(hiddens[axis], down_held[:, cols], preferred_element_type=jnp.float32)
                for cols in (upper, lower)
            ]
            answers[:, :, lanes(part, axis)] = halves(jnp.concatenate(result, axis=1))
        each_partner(lambda axis, p: send(
            answers.at[p, :, lanes(part, axis)], returned.at[index[axis], :, lanes(part, axis)],
            ret_send.at[part, axis], ret_recv.at[part, axis], in_plane(axis, p),
        ))
        for axis in axes:
            returned[index[axis], :, lanes(part, axis)] = answers[index[axis], :, lanes(part, axis)]

    for part in range(len(PARTS)):
        for axis in axes:
            wait(returned.at[many, :, lanes(part, axis)], ret_recv.at[part, axis])
            size = PARTS[part][axis][1]
            messages = returned[:, :, lanes(part, axis)].reshape(PLANE * 16, size)
            result = jnp.dot(weigh[axis], messages, preferred_element_type=jnp.float32)
            result = result.astype(jnp.bfloat16).reshape(2, SIDE, 16, size)
            upper, lower = both_columns(part, axis)
            partial[:, :, upper] = result[0]
            partial[:, :, lower] = result[1]
            if part == len(PARTS) - 1:
                own = along[axis]
                to_line(axis, lambda f: send(
                    partial.at[f, :, columns(axis)], landed.at[own, :, columns(axis)],
                    sum_send.at[axis, f], sum_recv.at[axis, own], on_line(axis, f),
                ))
    for axis in axes:
        to_line(axis, lambda f: wait(landed.at[0, :, columns(axis)], sum_recv.at[axis, f]))
        own = along[axis]
        block = partial[own, :, columns(axis)].astype(jnp.float32)
        for d in range(1, SIDE):
            block = block + landed[(own + d) % SIDE, :, columns(axis)].astype(jnp.float32)
        block = block + attended[:, columns(axis)].astype(jnp.float32)
        mixed[:, columns(axis)] = block.astype(jnp.bfloat16)

    wait(weight, head_weight_sems.at[1])
    for kv in range(2):
        loop(1, SIDE, lambda i: wait(heads.at[:, side(kv)], first_send.at[kv, (first + i) % SIDE]))
        for s in (before, after):
            loop(0, SIDE, lambda g: wait(heads.at[:, side(kv)], second_send.at[kv, s, g]))
        loop(0, SIDE, lambda g: wait(heads.at[:, side(kv)], relay_send.at[kv, g]))
    others_in_plane(lambda f, s: wait(products.at[s, f], back_send.at[s, f]))
    for axis in axes:
        to_line(axis, lambda f: wait(meta.at[axis, 0], meta_send.at[axis, f]))
        to_line(axis, lambda f: wait(landed.at[0, :, columns(axis)], share_send.at[axis, f]))
        to_line(axis, lambda f: wait(landed.at[0, :, columns(axis)], sum_send.at[axis, f]))
        for part in range(len(PARTS)):
            wait(picked.at[many, :, lanes(part, axis)], out_send.at[part, axis])
            wait(answers.at[many, :, lanes(part, axis)], ret_send.at[part, axis])


def local(
    residual,
    query,
    new_key_value,
    cached_key_rows,
    cached_value_rows,
    lengths,
    q_gain,
    k_gain,
    out_weight,
    moe_gain,
    expert_ids,
    gate_probs,
    expert_gate_up,
    expert_down,
):
    rows, width = residual.shape
    hidden = expert_down.shape[1]
    slots = cached_key_rows.shape[1]
    vmem = pl.BlockSpec(memory_space=pltpu.VMEM)
    hbm = pl.BlockSpec(memory_space=pltpu.HBM)
    sems = pltpu.SemaphoreType.DMA
    bf16 = jnp.bfloat16
    own = pltpu.VMEM((rows, width), bf16)
    caches = pltpu.VMEM(cached_key_rows.shape, bf16)
    messages = pltpu.VMEM((PLANE, 16, width // 2), bf16)
    lines = pltpu.VMEM((SIDE, rows, width), bf16)
    parts = len(PARTS)
    both = pl.pallas_call(
        kernel,
        out_shape=jax.ShapeDtypeStruct((2, rows, width), bf16),
        in_specs=[hbm] * 14,
        out_specs=vmem,
        scratch_shapes=[
            own,
            caches,
            caches,
            own,
            pltpu.VMEM(new_key_value.shape, bf16),
            pltpu.VMEM((1, rows), jnp.int32),
            pltpu.VMEM((1, 128), jnp.float32),
            pltpu.VMEM((1, 128), jnp.float32),
            pltpu.VMEM((1, width), jnp.float32),
            pltpu.VMEM((expert_ids.shape[1], rows), jnp.int32),
            pltpu.VMEM((expert_ids.shape[1], rows), jnp.float32),
            pltpu.VMEM((2, 256, slots), jnp.float32),
            pltpu.VMEM((256, 128), jnp.float32),
            own,
            pltpu.VMEM((width, 256), bf16),
            pltpu.VMEM((SIDE, SIDE, rows, width), bf16),
            pltpu.VMEM((SIDE, SIDE, rows, 256), bf16),
            own,
            own,
            pltpu.VMEM((width, 2 * hidden), bf16),
            pltpu.VMEM((hidden, width), bf16),
            pltpu.VMEM((3, SIDE, rows, 256), bf16),
            lines,
            messages,
            messages,
            pltpu.VMEM((256, width), bf16),
            pltpu.VMEM((256, 2 * hidden), jnp.float32),
            messages,
            messages,
            lines,
            lines,
            pltpu.VMEM((3, 256, SIDE * rows), bf16),
            pltpu.VMEM((3, 2 * SIDE * rows, 512), bf16),
            pltpu.VMEM((3, 256, 256), bf16),
            pltpu.VMEM((3, 256, 256), bf16),
            sems((11,)),
            sems((3,)),
            sems((2, SIDE)),
            sems((2, SIDE)),
            sems((2, SIDE, SIDE)),
            sems((2, SIDE, SIDE)),
            sems((2, SIDE)),
            sems((SIDE, SIDE)),
            sems((SIDE, SIDE)),
            sems((3 + 6 * parts,)),
            sems((3, SIDE)),
            sems((3, SIDE)),
            sems((3, SIDE)),
            sems((3, SIDE)),
            sems((parts, 3)),
            sems((parts, 3)),
            sems((parts, 3)),
            sems((parts, 3)),
            sems((3, SIDE)),
            sems((3, SIDE)),
        ],
        compiler_params=pltpu.CompilerParams(
            collective_id=1, has_side_effects=True, vmem_limit_bytes=60 << 20
        ),
        name="layer",
    )(
        residual, query, new_key_value, cached_key_rows, cached_value_rows,
        lengths.reshape(1, rows), q_gain.reshape(1, 128), k_gain.reshape(1, 128), out_weight,
        moe_gain.reshape(1, width), expert_ids.T, gate_probs.T, expert_gate_up, expert_down,
    )
    return (both[0], both[1])


def solution(mesh):
    return jax.shard_map(
        local,
        mesh=mesh,
        in_specs=(
            P(("dp", "ep"), None),
            P(("dp", "ep"), None),
            P(("dp", "ep"), None, None),
            P(("dp", "ep"), None, None),
            P(("dp", "ep"), None, None),
            P(("dp", "ep")),
            P(),
            P(),
            P(None, "ep"),
            P(),
            P(("dp", "ep"), None),
            P(("dp", "ep"), None),
            P(("dp", "ep"), None, None),
            P(("dp", "ep"), None, None),
        ),
        out_specs=(P(("dp", "ep"), None), P(("dp", "ep"), None)),
        check_vma=False,
    )
```
